32 devices in a mesh: dp: 4 (over z), seq: 8 (over y, x, core).
Axes of the slice: x: 2, y: 2, z: 4, core: 2. Of those that a mesh axis runs over, the one named last changes fastest.
Arguments:
- tokens: bfloat16 [4, 12288, 1024], P('dp', 'seq'), may hold values from -6 to 6
- image_tokens: bfloat16 [4, 1024, 768], P('dp', 'seq'), may hold values from -51 to 51
- norm_gain: float32 [1024], replicated, may hold values from 0.1 to 1.9
- w_query: bfloat16 [1024, 1024], replicated, may hold values from -0.1875 to 0.1875
- w_key: bfloat16 [768, 1024], replicated, may hold values from -0.21875 to 0.21875
- w_value: bfloat16 [768, 1024], replicated, may hold values from -0.21875 to 0.21875
- w_out: bfloat16 [1024, 1024], replicated, may hold values from -0.1875 to 0.1875
- w_plane: bfloat16 [1024, 80], replicated, may hold values from -0.1875 to 0.1875
- dec_w1: bfloat16 [64, 80], replicated, may hold values from -0.625 to 0.625
- dec_b1: float32 [64], replicated, may hold values from -3 to 3
- dec_w2: bfloat16 [64, 64], replicated, may hold values from -0.75 to 0.75
- dec_b2: float32 [64], replicated, may hold values from -3 to 3
- dec_w3: bfloat16 [4, 64], replicated, may hold values from -0.75 to 0.75
- dec_b3: float32 [4], replicated, may hold values from -3 to 3
- corner_idx: int32 [4, 12, 32768], P('dp', None, 'seq'), may hold values from 0 to 12287, as said below
- corner_wts: bfloat16 [4, 12, 32768], P('dp', None, 'seq'), may hold values from 0 to 1, as said below
- target_color: float32 [4, 3, 256], P('dp', None, 'seq'), may hold values from 0 to 1
Outputs:
- colors: float32 [4, 3, 256], P('dp', None, 'seq')
- token_grad: bfloat16 [4, 12288, 1024], P('dp', 'seq')
- plane_weight_grad: float32 [1024, 80], replicated
The draws below stay inside these ranges and needn't reach their ends.
Inputs may be any that keep to these rules, and one draw needn't show every extreme that they name: `corner_idx`: each entry names a triplane token of the scene; for each sample and plane the four entries are the corners of one grid cell of that plane, and consecutive samples of a ray walk through neighbouring cells. `corner_wts`: for each sample and plane the four weights are the bilinear weights of one point in that cell.
All inputs are finite; a program needn't handle non-finite values.
Results may differ from the reference program's by a relative error of at most 0.017.
Values may be sent and summed in bfloat16 or wider, within the bound.
No kernel may reach another device: no remote copies, remote signals or barrier semaphores. Data moves between devices by JAX's collectives and lax.ppermute only.
A program may use at most 128 MiB of HBM per device.

```python
import math
import jax
import jax.numpy as jnp
from jax import lax

D = 1024
HEADS = 16
C = 768
GRID = 64
CP = 80
HID = 64
STEPS = 128
SCENES = 4
TOK = 12288
NIMG = 1024
RAYS = 256


def sample_table(key):
    subkeys = jax.random.split(jax.random.fold_in(key, 11), 3)
    anchor = jax.random.randint(subkeys[0], (SCENES, RAYS, 1, 3), 0, GRID - 1)
    heading = jax.random.randint(subkeys[1], (SCENES, RAYS, 1, 3), -2, 3)
    step_ids = jnp.arange(STEPS, dtype=jnp.int32)[None, None, :, None]
    cell_ids = jnp.clip(anchor + step_ids * heading // 4, 0, GRID - 2)
    fraction = jax.random.uniform(subkeys[2], (SCENES, RAYS, STEPS, 3), jnp.float32)
    plane_axes = ((0, 1), (0, 2), (1, 2))
    index_list = []
    weight_list = []
    for plane_id in range(3):
        first_axis, second_axis = plane_axes[plane_id]
        for shift_b in (0, 1):
            for shift_a in (0, 1):
                flat_id = plane_id * GRID * GRID + (cell_ids[..., second_axis] + shift_b) * GRID + cell_ids[..., first_axis] + shift_a
                weight_a = fraction[..., first_axis] if shift_a else 1.0 - fraction[..., first_axis]
                weight_b = fraction[..., second_axis] if shift_b else 1.0 - fraction[..., second_axis]
                index_list.append(flat_id.reshape(SCENES, RAYS * STEPS))
                weight_list.append((weight_a * weight_b).reshape(SCENES, RAYS * STEPS))
    return (jnp.stack(index_list, axis=1).astype(jnp.int32), jnp.stack(weight_list, axis=1))


def draw_corner_idx(key, part):
    return sample_table(key)[0]


def draw_corner_wts(key, part):
    return sample_table(key)[1].astype(jnp.bfloat16)


def draw_image_tokens(key, part):
    subkeys = jax.random.split(jax.random.fold_in(key, 5), 1)
    base = jnp.clip(jax.random.normal(subkeys[0], (SCENES, NIMG, C), jnp.float32), -6.0, 6.0)
    return base.astype(jnp.bfloat16)


def steps_of(rng, extent, pieces, low, largest):
    loudness, own = 1.0, jax.random.fold_in(rng, 6)
    for dim, blocks in pieces:
        draws = jnp.exp(jax.random.uniform(jax.random.fold_in(own, dim), (blocks,), jnp.float32, low / len(pieces), largest / len(pieces)))
        loudness = loudness * jnp.repeat(draws, extent[dim] // blocks).reshape([-1 if axis == dim else 1 for axis in range(len(extent))])
    return loudness


def bell_draw(stream_key, shape, width, most, shards=(), kind=jnp.bfloat16):
    drawn = jax.random.normal(stream_key, shape, jnp.float32) * width
    if len(shards) > 0:
        drawn = steps_of(stream_key, shape, shards, -0.22, 0.18) * drawn
    return jnp.clip(drawn, min=-most, max=most).astype(kind)


def setup_inputs(seed: int = 0) -> dict:
    streams_of = jax.random.split(jax.random.key(seed), 18)
    tokens = bell_draw(streams_of[0], (SCENES, TOK, D), 1.0, 6.0, ((0, 4), (1, 8)))
    image_tokens = draw_image_tokens(jax.random.fold_in(streams_of[17], 71), 0)
    norm_gain = jnp.clip(1.0 + 0.18 * jax.random.normal(streams_of[2], (D,), jnp.float32), 0.1, 1.9)
    w_query = bell_draw(streams_of[3], (D, D), D ** -0.5, 0.1875)
    w_key = bell_draw(streams_of[4], (C, D), C ** -0.5, 0.21875)
    w_value = bell_draw(streams_of[5], (C, D), C ** -0.5, 0.21875)
    w_out = bell_draw(streams_of[6], (D, D), D ** -0.5, 0.1875)
    w_plane = bell_draw(streams_of[7], (D, CP), D ** -0.5, 0.1875)
    dec_w1 = bell_draw(streams_of[8], (HID, CP), CP ** -0.5, 0.625)
    dec_b1 = bell_draw(streams_of[9], (HID,), 0.5, 3.0, (), jnp.float32)
    dec_w2 = bell_draw(streams_of[10], (HID, HID), HID ** -0.5, 0.75)
    dec_b2 = bell_draw(streams_of[11], (HID,), 0.5, 3.0, (), jnp.float32)
    dec_w3 = bell_draw(streams_of[12], (4, HID), HID ** -0.5, 0.75)
    dec_b3 = bell_draw(streams_of[13], (4,), 0.5, 3.0, (), jnp.float32)
    corner_idx = draw_corner_idx(jax.random.fold_in(streams_of[17], 71), 0)
    corner_wts = draw_corner_wts(jax.random.fold_in(streams_of[17], 71), 0)
    target_color = jnp.clip(1.0 * jax.random.uniform(streams_of[16], (SCENES, 3, RAYS), jnp.float32) ** steps_of(streams_of[16], (SCENES, 3, RAYS), ((0, 4), (2, 8)), -0.2, 0.2), 0.0, 1.0)
    return {"tokens": tokens, "image_tokens": image_tokens, "norm_gain": norm_gain, "w_query": w_query, "w_key": w_key, "w_value": w_value, "w_out": w_out, "w_plane": w_plane, "dec_w1": dec_w1, "dec_b1": dec_b1, "dec_w2": dec_w2, "dec_b2": dec_b2, "dec_w3": dec_w3, "dec_b3": dec_b3, "corner_idx": corner_idx, "corner_wts": corner_wts, "target_color": target_color}


NORM_EPS = 1e-05
DEPTH_STEP = 0.02

def plain_norm(inputs):
    row_mean = lax.optimization_barrier(jnp.mean(inputs, axis=-1, keepdims=True))
    centred = inputs - row_mean
    row_var = lax.optimization_barrier(jnp.mean(centred * centred, axis=-1, keepdims=True))
    return centred * lax.rsqrt(row_var + NORM_EPS)

def render(features, dec_w1, dec_b1, dec_w2, dec_b2, dec_w3, dec_b3):
    hidden = jax.nn.silu(jnp.dot(dec_w1, features, preferred_element_type=jnp.float32) + dec_b1[:, None]).astype(jnp.bfloat16)
    hidden = jax.nn.silu(jnp.dot(dec_w2, hidden, preferred_element_type=jnp.float32) + dec_b2[:, None]).astype(jnp.bfloat16)
    decoded = jnp.dot(dec_w3, hidden, preferred_element_type=jnp.float32) + dec_b3[:, None]
    optical = jax.nn.softplus(decoded[0]).reshape(-1, STEPS) * DEPTH_STEP
    albedo = jax.nn.sigmoid(decoded[1:4]).reshape(3, -1, STEPS)
    before = jnp.cumsum(optical, axis=1) - optical
    weight = jnp.exp(-before) * (1.0 - jnp.exp(-optical))
    return lax.optimization_barrier(jnp.sum(weight[None] * albedo, axis=2))

def reference(tokens, image_tokens, norm_gain, w_query, w_key, w_value, w_out, w_plane, dec_w1, dec_b1, dec_w2, dec_b2, dec_w3, dec_b3, corner_idx, corner_wts, target_color):
    head_dim = D // HEADS
    score_scale = 1.0 / math.sqrt(head_dim)

    def scene(parts):
        own_tokens, images, index_table, weight_table, target = parts
        normed = plain_norm(own_tokens.astype(jnp.float32)).astype(jnp.bfloat16)
        queries = jnp.dot(normed, w_query, preferred_element_type=jnp.float32).astype(jnp.bfloat16)
        key_rows = jnp.dot(images, w_key, preferred_element_type=jnp.float32).astype(jnp.bfloat16)
        values = jnp.dot(images, w_value, preferred_element_type=jnp.float32).astype(jnp.bfloat16)
        query_heads = queries.reshape(TOK, HEADS, head_dim).transpose(1, 0, 2)
        key_heads = key_rows.reshape(NIMG, HEADS, head_dim).transpose(1, 0, 2)
        value_heads = values.reshape(NIMG, HEADS, head_dim).transpose(1, 0, 2)

        def one_head(head_parts):
            query_one, key_one, value_one = head_parts
            scores = jnp.dot(query_one, key_one.T, preferred_element_type=jnp.float32) * score_scale
            row_max = lax.optimization_barrier(jnp.max(scores, axis=1, keepdims=True))
            exp_terms = jnp.exp(scores - row_max)
            prob_sum = lax.optimization_barrier(jnp.sum(exp_terms, axis=1, keepdims=True))
            return jnp.dot(exp_terms.astype(jnp.bfloat16), value_one, preferred_element_type=jnp.float32) / prob_sum
        head_out = lax.map(one_head, (query_heads, key_heads, value_heads))
        attended = head_out.transpose(1, 0, 2).reshape(TOK, D).astype(jnp.bfloat16)
        mixed = (own_tokens.astype(jnp.float32) + jnp.dot(attended, w_out, preferred_element_type=jnp.float32)).astype(jnp.bfloat16)
        plane_in = (plain_norm(mixed.astype(jnp.float32)) * norm_gain).astype(jnp.bfloat16)
        planes = jnp.dot(w_plane.T, plane_in.T, preferred_element_type=jnp.float32).astype(jnp.bfloat16)
        picked = planes[:, index_table].astype(jnp.float32)
        features = lax.optimization_barrier(jnp.sum(picked * weight_table.astype(jnp.float32)[None], axis=1)).astype(jnp.bfloat16)

        def shade_rays(feature_in):
            return render(feature_in, dec_w1, dec_b1, dec_w2, dec_b2, dec_w3, dec_b3)
        colors, pullback = jax.vjp(shade_rays, features)
        feat_grad = pullback(colors - target)[0].astype(jnp.bfloat16)
        grad_terms = (feat_grad.astype(jnp.float32)[:, None, :] * weight_table.astype(jnp.float32)[None]).reshape(CP, -1)
        plane_grad = jnp.zeros((CP, TOK), jnp.float32).at[:, index_table.reshape(-1)].add(grad_terms)
        plane_grad = plane_grad.astype(jnp.bfloat16)
        weight_grad = jnp.dot(plane_in.T, plane_grad.T, preferred_element_type=jnp.float32)
        token_grad = jnp.dot(plane_grad.T, w_plane.T, preferred_element_type=jnp.float32).astype(jnp.bfloat16)
        return (colors, token_grad, weight_grad)
    colors, token_grad, weight_grad = lax.map(scene, (tokens, image_tokens, corner_idx, corner_wts, target_color))
    return (colors, token_grad, lax.optimization_barrier(jnp.sum(weight_grad, axis=0)))
```

```python
import functools
import math

import jax
import jax.numpy as jnp
from jax import lax
from jax.experimental import pallas as pl
from jax.experimental.pallas import tpu as pltpu
from jax.sharding import PartitionSpec as P

HEADS = 16
STEPS = 128
PLANES = 3
LANES = 128

NORM_EPS = 1e-05
DEPTH_STEP = 0.02
VMEM_BYTES = 56 * 1024 * 1024

F32 = jnp.float32
BF16 = jnp.bfloat16


def contract(left, right, left_dim, right_dim, out_type=F32, precision=None):
    return lax.dot_general(
        left,
        right,
        (((left_dim,), (right_dim,)), ((), ())),
        preferred_element_type=out_type,
        precision=precision,
    )


def plain_norm(inputs):
    row_mean = jnp.mean(inputs, axis=-1, keepdims=True)
    centred = inputs - row_mean
    row_var = jnp.mean(centred * centred, axis=-1, keepdims=True)
    return centred * lax.rsqrt(row_var + NORM_EPS)


def params(steps=1):
    return pltpu.CompilerParams(
        vmem_limit_bytes=VMEM_BYTES, dimension_semantics=("arbitrary",) * steps
    )


def swap(array, axis, distance):
    pairs = [(i, i ^ distance) for i in range(lax.axis_size(axis))]
    return lax.ppermute(array, axis, pairs)


def gather_scene(piece):
    far = [piece] + [swap(piece, "seq", k) for k in range(2, lax.axis_size("seq"), 2)]
    pieces = []
    for own_side in far:
        pieces += [own_side, swap(own_side, "seq", 1)]
    return pieces


def whole(shape):
    return pl.BlockSpec(shape, lambda step: (0,) * len(shape))


def query_kernel(query_scale, tokens_ref, w_query_ref, queries_ref):
    normed = plain_norm(tokens_ref[...].astype(F32)).astype(BF16)
    queries = jnp.dot(normed, w_query_ref[...], preferred_element_type=F32)
    queries_ref[...] = (queries * query_scale).astype(BF16)


def query_call(tokens, w_query, query_scale):
    rows, width = tokens.shape
    tile = math.gcd(rows, 512)
    return pl.pallas_call(
        functools.partial(query_kernel, query_scale),
        grid=(rows // tile,),
        in_specs=[pl.BlockSpec((tile, width), lambda step: (step, 0)), whole(w_query.shape)],
        out_specs=pl.BlockSpec((tile, width), lambda step: (step, 0)),
        out_shape=jax.ShapeDtypeStruct((rows, width), BF16),
        compiler_params=params(),
        name="queries",
    )(tokens, w_query)


def keys_kernel(count, *refs):
    images_refs, (w_key_ref, w_value_ref, keys_ref, values_ref) = refs[:count], refs[count:]
    images = jnp.concatenate([ref[...] for ref in images_refs], axis=0)
    keys = jnp.dot(images, w_key_ref[...], preferred_element_type=F32).astype(BF16)
    keys_ref[...] = keys.T
    values = jnp.dot(images, w_value_ref[...], preferred_element_type=F32).astype(BF16)
    ones = jnp.ones((values.shape[0], LANES), BF16)
    for group in range(values.shape[1] // LANES):
        values_ref[group, :, :LANES] = values[:, group * LANES : (group + 1) * LANES]
        values_ref[group, :, LANES:] = ones


def keys_call(images, w_key, w_value):
    rows = sum(piece.shape[0] for piece in images)
    width = w_key.shape[1]
    return pl.pallas_call(
        functools.partial(keys_kernel, len(images)),
        out_shape=[
            jax.ShapeDtypeStruct((width, rows), BF16),
            jax.ShapeDtypeStruct((width // LANES, rows, 2 * LANES), BF16),
        ],
        compiler_params=pltpu.CompilerParams(vmem_limit_bytes=VMEM_BYTES),
        name="keys_values",
    )(*images, w_key, w_value)


def attend_kernel(
    head_dim,
    tokens_ref,
    queries_ref,
    keys_ref,
    values_ref,
    w_out_ref,
    gain_ref,
    w_plane_ref,
    plane_in_ref,
    planes_ref,
    attended_ref,
):
    rows, width = tokens_ref.shape
    lane_ids = lax.broadcasted_iota(jnp.int32, (rows, LANES), 1)

    def group_step(group, _):
        start = pl.multiple_of(group * LANES, LANES)
        columns = pl.ds(start, LANES)
        group_queries = queries_ref[:, columns]
        group_keys = keys_ref[columns, :]
        group_values = values_ref[group]
        joined = jnp.zeros((rows, LANES), F32)
        for low in range(0, LANES, head_dim):
            own = (lane_ids >= low) & (lane_ids < low + head_dim)
            head_queries = jnp.where(own, group_queries, jnp.zeros_like(group_queries))
            scores = jnp.dot(head_queries, group_keys, preferred_element_type=F32)
            row_max = jnp.max(scores, axis=1, keepdims=True)
            probs = jnp.exp2(scores - row_max).astype(BF16)
            sums = jnp.dot(probs, group_values, preferred_element_type=F32)
            joined = jnp.where(own, sums[:, :LANES] / sums[:, LANES:], joined)
        attended_ref[:, columns] = joined.astype(BF16)
        return 0

    lax.fori_loop(0, width // LANES, group_step, 0)
    mixed = (
        tokens_ref[...].astype(F32)
        + jnp.dot(attended_ref[...], w_out_ref[...], preferred_element_type=F32)
    ).astype(BF16)
    plane_in = (plain_norm(mixed.astype(F32)) * gain_ref[...]).astype(BF16)
    plane_in_ref[...] = plane_in
    planes_ref[...] = contract(w_plane_ref[...], plane_in, 1, 1).astype(BF16)


def attend_call(tokens, queries, keys, values, w_out, norm_gain, w_plane_t, head_dim):
    rows, width = tokens.shape
    channels = w_plane_t.shape[0]
    tile = math.gcd(rows, 768)
    row_block = pl.BlockSpec((tile, width), lambda step: (step, 0))
    return pl.pallas_call(
        functools.partial(attend_kernel, head_dim),
        grid=(rows // tile,),
        in_specs=[
            row_block,
            row_block,
            whole(keys.shape),
            whole(values.shape),
            whole(w_out.shape),
            whole((1, width)),
            whole(w_plane_t.shape),
        ],
        out_specs=[row_block, pl.BlockSpec((channels, tile), lambda step: (0, step))],
        out_shape=[
            jax.ShapeDtypeStruct((rows, width), BF16),
            jax.ShapeDtypeStruct((channels, rows), BF16),
        ],
        scratch_shapes=[pltpu.VMEM((tile, width), BF16)],
        compiler_params=params(),
        name="attention_planes",
    )(tokens, queries, keys, values, w_out, norm_gain.reshape(1, width), w_plane_t)


def shifted_left(block, lanes):
    return pltpu.roll(block, block.shape[1] - lanes, 1) if lanes else block


def render_kernel(
    grid_side,
    row_span,
    shares,
    *refs,
):
    piece_refs, refs = refs[:shares], refs[shares:]
    (index_ref, weight_ref, target_ref, w1_ref, b1_ref, w2_ref, b2_ref, w3_ref, b3_ref), refs = (
        refs[:9],
        refs[9:],
    )
    colors_ref, even_refs, odd_refs = refs[0], refs[1 : 1 + shares // 2], refs[1 + shares // 2 : 1 + shares]
    bands_ref, sums_ref, matrix_ref, whole_ref = refs[1 + shares :]
    step = pl.program_id(0)
    me = lax.axis_index("seq")
    channels, share = piece_refs[0].shape
    samples = index_ref.shape[1]
    corners = index_ref.shape[0]
    plane_size = grid_side * grid_side
    band_rows = row_span + 1
    band = band_rows * grid_side
    stride = row_span * grid_side
    bands = (grid_side - 1) // row_span
    rays = samples // STEPS

    @pl.when(step == 0)
    def fill_bands():
        sums_ref[...] = jnp.zeros_like(sums_ref)
        for k in range(shares):
            whole_ref[me ^ k] = piece_refs[k][...]
        whole_planes = jnp.concatenate([whole_ref[i] for i in range(shares)], axis=1)
        for plane in range(PLANES):
            for q in range(bands):
                start = plane * plane_size + q * stride
                lead = start % LANES
                extent = band + (LANES if lead else 0)
                piece = whole_planes[:, start - lead : start - lead + extent]
                if lead:
                    piece = shifted_left(piece.astype(F32), lead).astype(BF16)
                bands_ref[plane, q * channels : (q + 1) * channels, :] = piece[:, :band]

    index = index_ref[...]
    weights = weight_ref[...].astype(F32)
    features = jnp.zeros((channels, samples), F32)
    x_ids = lax.broadcasted_iota(jnp.int32, (grid_side, samples), 0)
    band_ids = []
    for plane in range(PLANES):
        in_plane = (index >= plane * plane_size) & (index < (plane + 1) * plane_size)
        base = jnp.min(jnp.where(in_plane, index, PLANES * plane_size), axis=0, keepdims=True)
        picked = [
            jnp.sum(jnp.where(index == base + shift, weights, 0.0), axis=0, keepdims=True)
            for shift in (0, 1, grid_side, grid_side + 1)
        ]
        local = base - plane * plane_size
        first_row = local // grid_side
        first_x = local - first_row * grid_side
        band_id = first_row // row_span
        band_row = first_row - band_id * row_span
        band_ids.append(band_id)
        at_first = x_ids == first_x
        at_second = x_ids == first_x + 1
        upper = jnp.where(at_first, picked[0], jnp.where(at_second, picked[1], 0.0)).astype(BF16)
        lower = jnp.where(at_first, picked[2], jnp.where(at_second, picked[3], 0.0)).astype(BF16)
        row_marks = [
            jnp.where(band_row == r, 1.0, 0.0).astype(BF16) for r in range(row_span)
        ]
        for r in range(band_rows):
            block = None
            if r < row_span:
                block = upper * row_marks[r]
            if r > 0:
                below = lower * row_marks[r - 1]
                block = below if block is None else block + below
            matrix_ref[plane, r * grid_side : (r + 1) * grid_side, :] = block
        products = jnp.dot(bands_ref[plane], matrix_ref[plane], preferred_element_type=F32)
        for q in range(bands):
            features = features + jnp.where(
                band_id == q, products[q * channels : (q + 1) * channels, :], 0.0
            )
    features = features.astype(BF16)

    pre1 = jnp.dot(w1_ref[...], features, preferred_element_type=F32) + b1_ref[...]
    gate1 = jax.nn.sigmoid(pre1)
    hidden1 = (pre1 * gate1).astype(BF16)
    pre2 = jnp.dot(w2_ref[...], hidden1, preferred_element_type=F32) + b2_ref[...]
    gate2 = jax.nn.sigmoid(pre2)
    hidden2 = (pre2 * gate2).astype(BF16)
    decoded = jnp.dot(w3_ref[...], hidden2, preferred_element_type=F32) + b3_ref[...]

    def by_ray(row):
        return jnp.concatenate(
            [decoded[row : row + 1, i * STEPS : (i + 1) * STEPS] for i in range(rays)], axis=0
        )

    def along_lanes(by_rays):
        return jnp.concatenate([by_rays[i : i + 1, :] for i in range(rays)], axis=1)

    earlier = lax.broadcasted_iota(jnp.int32, (STEPS, STEPS), 0)
    later = lax.broadcasted_iota(jnp.int32, (STEPS, STEPS), 1)
    raw_density = by_ray(0)
    density = jnp.maximum(raw_density, 0.0) + jnp.log1p(jnp.exp(-jnp.abs(raw_density)))
    optical = density * DEPTH_STEP
    before = jnp.dot(
        optical,
        jnp.where(earlier < later, 1.0, 0.0),
        preferred_element_type=F32,
        precision=lax.Precision.HIGHEST,
    )
    through = jnp.exp(-before)
    passing = jnp.exp(-optical)
    ray_weight = through * (1.0 - passing)
    target = target_ref[...]
    lane_ids = lax.broadcasted_iota(jnp.int32, (rays, LANES), 1)
    color_block = jnp.zeros((rays, LANES), F32)
    weight_slope = jnp.zeros((rays, STEPS), F32)
    decoded_slopes = []
    for channel in range(3):
        albedo = jax.nn.sigmoid(by_ray(1 + channel))
        color = jnp.sum(ray_weight * albedo, axis=1, keepdims=True)
        color_block = jnp.where(lane_ids == channel, color, color_block)
        residual = color - jnp.sum(
            jnp.where(lane_ids == channel, target, 0.0), axis=1, keepdims=True
        )
        weight_slope = weight_slope + residual * albedo
        decoded_slopes.append(along_lanes(residual * ray_weight * albedo * (1.0 - albedo)))
    colors_ref[...] = color_block
    behind = jnp.dot(
        weight_slope * ray_weight,
        jnp.where(earlier > later, 1.0, 0.0),
        preferred_element_type=F32,
        precision=lax.Precision.HIGHEST,
    )
    optical_slope = weight_slope * through * passing - behind
    density_slope = optical_slope * DEPTH_STEP * jax.nn.sigmoid(raw_density)
    decoded_slope = jnp.concatenate([along_lanes(density_slope)] + decoded_slopes, axis=0)

    hidden2_slope = contract(w3_ref[...], decoded_slope.astype(BF16), 0, 0).astype(BF16)
    pre2_slope = hidden2_slope.astype(F32) * (gate2 * (1.0 + pre2 * (1.0 - gate2)))
    hidden1_slope = contract(w2_ref[...], pre2_slope.astype(BF16), 0, 0).astype(BF16)
    pre1_slope = hidden1_slope.astype(F32) * (gate1 * (1.0 + pre1 * (1.0 - gate1)))
    feature_slope = contract(w1_ref[...], pre1_slope.astype(BF16), 0, 0).astype(BF16)

    for plane in range(PLANES):
        spread = jnp.concatenate(
            [
                feature_slope * jnp.where(band_ids[plane] == q, 1.0, 0.0).astype(BF16)
                for q in range(bands)
            ],
            axis=0,
        )
        sums_ref[plane] += contract(spread, matrix_ref[plane], 1, 1)

    @pl.when(step == pl.num_programs(0) - 1)
    def join_bands():
        joined = []
        for plane in range(PLANES):
            total = jnp.zeros((channels, plane_size), F32)
            for q in range(bands):
                start = q * stride
                lead = start % LANES
                piece = sums_ref[plane, q * channels : (q + 1) * channels, :]
                if lead:
                    piece = jnp.concatenate([piece, jnp.zeros((channels, LANES), F32)], axis=1)
                    piece = pltpu.roll(piece, lead, 1)
                parts = []
                if start - lead > 0:
                    parts.append(jnp.zeros((channels, start - lead), F32))
                parts.append(piece)
                left_over = plane_size - (start - lead) - piece.shape[1]
                if left_over > 0:
                    parts.append(jnp.zeros((channels, left_over), F32))
                total = total + jnp.concatenate(parts, axis=1)
            joined.append(total.astype(BF16))
        joined = jnp.concatenate(joined, axis=1)
        for i in range(shares):
            whole_ref[i] = joined[:, i * share : (i + 1) * share]
        for k in range(0, shares, 2):
            even_refs[k // 2][...] = whole_ref[me ^ k]
            odd_refs[k // 2][...] = whole_ref[me ^ (k + 1)]


def render_call(pieces, index, weights, target, w1, b1, w2, b2, w3, b3):
    shares = len(pieces)
    channels, share = pieces[0].shape
    corners, samples = index.shape
    grid_side = math.isqrt(shares * share // PLANES)
    row_span = next(
        span
        for span in range(7, 0, -1)
        if (grid_side - 1) % span == 0
    )
    bands = (grid_side - 1) // row_span
    band = (row_span + 1) * grid_side
    rays = samples // STEPS
    tile_rays = math.gcd(rays, 8)
    tile = tile_rays * STEPS
    padded_target = jnp.pad(target.T, ((0, 0), (0, LANES - target.shape[0])))
    column = lambda array: array.reshape(-1, 1)
    colors, *grads = pl.pallas_call(
        functools.partial(render_kernel, grid_side, row_span, shares),
        grid=(rays // tile_rays,),
        in_specs=[
            *[whole((channels, share))] * shares,
            pl.BlockSpec((corners, tile), lambda step: (0, step)),
            pl.BlockSpec((corners, tile), lambda step: (0, step)),
            pl.BlockSpec((tile_rays, LANES), lambda step: (step, 0)),
            whole(w1.shape),
            whole((w1.shape[0], 1)),
            whole(w2.shape),
            whole((w2.shape[0], 1)),
            whole(w3.shape),
            whole((w3.shape[0], 1)),
        ],
        out_specs=[
            pl.BlockSpec((tile_rays, LANES), lambda step: (step, 0)),
            *[whole((channels, share))] * shares,
        ],
        out_shape=[
            jax.ShapeDtypeStruct((rays, LANES), F32),
            *[jax.ShapeDtypeStruct((channels, share), BF16)] * shares,
        ],
        scratch_shapes=[
            pltpu.VMEM((PLANES, bands * channels, band), BF16),
            pltpu.VMEM((PLANES, bands * channels, band), F32),
            pltpu.VMEM((PLANES, band, tile), BF16),
            pltpu.VMEM((shares, channels, share), BF16),
        ],
        compiler_params=params(),
        name="render",
    )(*pieces, index, weights, padded_target, w1, column(b1), w2, column(b2), w3, column(b3))
    return colors[:, : target.shape[0]].T, grads[: shares // 2], grads[shares // 2 :]


def weight_grad_kernel(count, *refs):
    part_refs, (plane_in_ref, even_ref, odd_ref, grad_ref, chunk_ref) = refs[:count], refs[count:]
    me = lax.axis_index("seq")
    grad = part_refs[0][...].astype(F32)
    for ref in part_refs[1:]:
        grad = grad + ref[...].astype(F32)
    grad = grad.astype(BF16)
    grad_ref[...] = grad
    total = jnp.dot(grad, plane_in_ref[...], preferred_element_type=F32)
    shares, _, columns = chunk_ref.shape
    for i in range(shares):
        chunk_ref[i] = total[:, i * columns : (i + 1) * columns]
    for j in range(shares // 2):
        even_ref[j] = chunk_ref[me ^ (2 * j)]
        odd_ref[j] = chunk_ref[me ^ (2 * j + 1)]


def weight_grad_call(parts, plane_in, shares):
    rows, width = plane_in.shape
    channels = parts[0].shape[0]
    columns = width // shares
    chunks = (shares // 2, channels, columns)
    return pl.pallas_call(
        functools.partial(weight_grad_kernel, len(parts)),
        out_shape=[
            jax.ShapeDtypeStruct(chunks, F32),
            jax.ShapeDtypeStruct(chunks, F32),
            jax.ShapeDtypeStruct((channels, rows), BF16),
        ],
        scratch_shapes=[pltpu.VMEM((shares, channels, columns), F32)],
        compiler_params=pltpu.CompilerParams(vmem_limit_bytes=VMEM_BYTES),
        name="weight_grad",
    )(*parts, plane_in)


def token_grad_kernel(grad_ref, w_plane_ref, token_grad_ref):
    token_grad_ref[...] = contract(grad_ref[...], w_plane_ref[...], 0, 0).astype(BF16)


def token_grad_call(grad, w_plane_t):
    channels, rows = grad.shape
    width = w_plane_t.shape[1]
    tile = math.gcd(rows, 384)
    return pl.pallas_call(
        token_grad_kernel,
        grid=(rows // tile,),
        in_specs=[
            pl.BlockSpec((channels, tile), lambda step: (0, step)),
            whole(w_plane_t.shape),
        ],
        out_specs=pl.BlockSpec((tile, width), lambda step: (step, 0)),
        out_shape=jax.ShapeDtypeStruct((rows, width), BF16),
        cost_estimate=pl.CostEstimate(
            flops=2 * rows * width * channels, bytes_accessed=2 * rows * width, transcendentals=0
        ),
        compiler_params=params(),
        name="token_grad",
    )(grad, w_plane_t)


def join_kernel(count, *refs):
    chunk_refs, (out_ref,) = refs[:count], refs[count:]
    me = lax.axis_index("seq")
    columns = chunk_refs[0].shape[1]
    for k in range(count):
        start = pl.multiple_of((me ^ k) * columns, columns)
        out_ref[pl.ds(start, columns), :] = chunk_refs[k][...].T


def join_call(chunks):
    channels, columns = chunks[0].shape
    return pl.pallas_call(
        functools.partial(join_kernel, len(chunks)),
        out_shape=jax.ShapeDtypeStruct((columns * len(chunks), channels), F32),
        name="join_weight_grad",
    )(*chunks)


def body(
    tokens,
    image_tokens,
    norm_gain,
    w_query,
    w_key,
    w_value,
    w_out,
    w_plane,
    dec_w1,
    dec_b1,
    dec_w2,
    dec_b2,
    dec_w3,
    dec_b3,
    corner_idx,
    corner_wts,
    target_color,
):
    own_tokens = tokens[0]
    head_dim = own_tokens.shape[1] // HEADS
    query_scale = math.log2(math.e) / math.sqrt(head_dim)
    shares = lax.axis_size("seq")
    images = gather_scene(image_tokens[0])
    queries = query_call(own_tokens, w_query, query_scale)
    keys, values = keys_call(images, w_key, w_value)
    w_plane_t = w_plane.T
    plane_in, planes = attend_call(
        own_tokens, queries, keys, values, w_out, norm_gain, w_plane_t, head_dim
    )
    colors, kept, passed = render_call(
        gather_scene(planes),
        corner_idx[0],
        corner_wts[0],
        target_color[0],
        dec_w1,
        dec_b1,
        dec_w2,
        dec_b2,
        dec_w3,
        dec_b3,
    )
    parts = []
    for j in reversed(range(shares // 2)):
        pair = (kept[j].astype(F32) + swap(passed[j], "seq", 1).astype(F32)).astype(BF16)
        parts.append(swap(pair, "seq", 2 * j) if j else pair)
    kept, passed, grad = weight_grad_call(parts, plane_in, shares)
    token_grad = token_grad_call(grad, w_plane_t)
    pairs = kept + swap(passed, "seq", 1)
    chunk = pairs[0]
    for j in range(1, shares // 2):
        chunk = chunk + swap(pairs[j], "seq", 2 * j)
    scenes = chunk
    for k in range(1, lax.axis_size("dp")):
        scenes = scenes + swap(chunk, "dp", k)
    weight_grad = join_call(gather_scene(scenes))
    return (colors[None], token_grad[None], weight_grad)


def solution(mesh):
    in_specs = (
        P("dp", "seq", None),
        P("dp", "seq", None),
        P(),
        P(),
        P(),
        P(),
        P(),
        P(),
        P(),
        P(),
        P(),
        P(),
        P(),
        P(),
        P("dp", None, "seq"),
        P("dp", None, "seq"),
        P("dp", None, "seq"),
    )
    out_specs = (P("dp", None, "seq"), P("dp", "seq", None), P())
    return jax.shard_map(body, mesh=mesh, in_specs=in_specs, out_specs=out_specs, check_vma=False)
```

```python
import functools
import math

import jax
import jax.numpy as jnp
from jax import lax
from jax.experimental import pallas as pl
from jax.experimental.pallas import tpu as pltpu
from jax.sharding import PartitionSpec as P

HEADS = 16
STEPS = 128
PLANES = 3
LANES = 128
TILE_RAYS = 32

NORM_EPS = 1e-05
DEPTH_STEP = 0.02
MIB = 1024 * 1024
VMEM_BYTES = 56 * MIB

F32 = jnp.float32
BF16 = jnp.bfloat16


def contract(left, right, left_dim, right_dim, out_type=F32, precision=None):
    return lax.dot_general(
        left,
        right,
        (((left_dim,), (right_dim,)), ((), ())),
        preferred_element_type=out_type,
        precision=precision,
    )


def plain_norm(inputs):
    row_mean = jnp.mean(inputs, axis=-1, keepdims=True)
    centred = inputs - row_mean
    row_var = jnp.mean(centred * centred, axis=-1, keepdims=True)
    return centred * lax.rsqrt(row_var + NORM_EPS)


def params(vmem_bytes=VMEM_BYTES):
    return pltpu.CompilerParams(vmem_limit_bytes=vmem_bytes)


def swap(array, axis, distance):
    pairs = [(i, i ^ distance) for i in range(lax.axis_size(axis))]
    return lax.ppermute(array, axis, pairs)


def from_chips(piece):
    return [swap(piece, "seq", k) for k in range(2, lax.axis_size("seq"), 2)]


def with_other_core(pieces):
    return [each for piece in pieces for each in (piece, swap(piece, "seq", 1))]


def gather_scene(piece):
    return with_other_core([piece]) + with_other_core(from_chips(piece))


def whole(shape):
    return pl.BlockSpec(shape, lambda step: (0,) * len(shape), pipeline_mode=pl.Buffered(1))


def kept(shape):
    return pl.BlockSpec(shape, lambda step: (0,) * len(shape))


def estimate(flops, bytes_accessed):
    return pl.CostEstimate(flops=flops, bytes_accessed=bytes_accessed, transcendentals=0)


def query_kernel(query_scale, tokens_ref, w_query_ref, queries_ref):
    normed = plain_norm(tokens_ref[...].astype(F32)).astype(BF16)
    queries = jnp.dot(normed, w_query_ref[...], preferred_element_type=F32)
    queries_ref[...] = (queries * query_scale).astype(BF16)


def query_call(tokens, w_query, query_scale):
    rows, width = tokens.shape
    tile = math.gcd(rows, 512)
    return pl.pallas_call(
        functools.partial(query_kernel, query_scale),
        grid=(rows // tile,),
        in_specs=[pl.BlockSpec((tile, width), lambda step: (step, 0)), whole(w_query.shape)],
        out_specs=pl.BlockSpec((tile, width), lambda step: (step, 0)),
        out_shape=jax.ShapeDtypeStruct((rows, width), BF16),
        cost_estimate=estimate(2 * rows * width * width, 4 * rows * width),
        compiler_params=params(32 * MIB),
        name="queries",
    )(tokens, w_query)


def attend_kernel(head_dim, shares, *refs):
    image_refs, refs = refs[:shares], refs[shares:]
    w_key_ref, w_value_ref, tokens_ref, queries_ref, w_out_ref, gain_ref, w_plane_ref = refs[:7]
    plane_in_ref, planes_ref, keys_ref, values_ref, attended_ref = refs[7:]
    rows, width = tokens_ref.shape
    groups = width // LANES

    @pl.when(pl.program_id(0) == 0)
    def project_images():
        images = jnp.concatenate([ref[...] for ref in image_refs], axis=0)
        keys = jnp.dot(images, w_key_ref[...], preferred_element_type=F32).astype(BF16)
        keys_ref[...] = keys.T
        values = jnp.dot(images, w_value_ref[...], preferred_element_type=F32).astype(BF16)
        ones = jnp.ones((values.shape[0], LANES), BF16)
        for group in range(groups):
            values_ref[group, :, :LANES] = values[:, group * LANES : (group + 1) * LANES]
            values_ref[group, :, LANES:] = ones

    lane_ids = lax.broadcasted_iota(jnp.int32, (rows, LANES), 1)
    heads = [(group, low) for group in range(groups) for low in range(0, LANES, head_dim)]

    def own_lanes(low):
        return (lane_ids >= low) & (lane_ids < low + head_dim)

    def head_scores(head):
        group, low = heads[head]
        group_queries = queries_ref[:, group * LANES : (group + 1) * LANES]
        head_queries = jnp.where(own_lanes(low), group_queries, jnp.zeros_like(group_queries))
        group_keys = keys_ref[group * LANES : (group + 1) * LANES, :]
        return jnp.dot(head_queries, group_keys, preferred_element_type=F32)

    upcoming = head_scores(0)
    joined = None
    for head, (group, low) in enumerate(heads):
        scores = upcoming
        if head + 1 < len(heads):
            upcoming = head_scores(head + 1)
        row_max = jnp.max(scores, axis=1, keepdims=True)
        probs = jnp.exp2(scores - row_max).astype(BF16)
        sums = jnp.dot(probs, values_ref[group], preferred_element_type=F32)
        head_out = sums[:, :LANES] / sums[:, LANES:]
        joined = head_out if low == 0 else jnp.where(own_lanes(low), head_out, joined)
        if low + head_dim == LANES:
            attended_ref[:, group * LANES : (group + 1) * LANES] = joined.astype(BF16)

    mixed = (
        tokens_ref[...].astype(F32)
        + jnp.dot(attended_ref[...], w_out_ref[...], preferred_element_type=F32)
    ).astype(BF16)
    plane_in = (plain_norm(mixed.astype(F32)) * gain_ref[...]).astype(BF16)
    plane_in_ref[...] = plane_in
    planes_ref[...] = contract(w_plane_ref[...], plane_in, 1, 1).astype(BF16)


def attend_call(images, w_key, w_value, tokens, queries, w_out, norm_gain, w_plane_t, head_dim):
    rows, width = tokens.shape
    channels = w_plane_t.shape[0]
    image_rows = sum(piece.shape[0] for piece in images)
    tile = math.gcd(rows, 768)
    row_block = pl.BlockSpec((tile, width), lambda step: (step, 0))
    return pl.pallas_call(
        functools.partial(attend_kernel, head_dim, len(images)),
        grid=(rows // tile,),
        in_specs=[
            *[whole(piece.shape) for piece in images],
            whole(w_key.shape),
            whole(w_value.shape),
            row_block,
            row_block,
            whole(w_out.shape),
            whole((1, width)),
            whole(w_plane_t.shape),
        ],
        out_specs=[row_block, pl.BlockSpec((channels, tile), lambda step: (0, step))],
        out_shape=[
            jax.ShapeDtypeStruct((rows, width), BF16),
            jax.ShapeDtypeStruct((channels, rows), BF16),
        ],
        scratch_shapes=[
            pltpu.VMEM((width, image_rows), BF16),
            pltpu.VMEM((width // LANES, image_rows, 2 * LANES), BF16),
            pltpu.VMEM((tile, width), BF16),
        ],
        cost_estimate=estimate(4 * rows * width * (image_rows + width // 2), 2 * rows * width),
        compiler_params=params(),
        name="attention_planes",
    )(*images, w_key, w_value, tokens, queries, w_out, norm_gain.reshape(1, width), w_plane_t)


def shifted_left(block, lanes):
    return pltpu.roll(block, block.shape[1] - lanes, 1) if lanes else block


def render_kernel(grid_side, row_span, shares, tile, *refs):
    piece_refs, refs = refs[:shares], refs[shares:]
    (index_ref, weight_ref, target_ref, w1_ref, b1_ref, w2_ref, b2_ref, w3_ref, b3_ref), refs = (
        refs[:9],
        refs[9:],
    )
    colors_ref, even_refs, odd_refs = (
        refs[0],
        refs[1 : 1 + shares // 2],
        refs[1 + shares // 2 : 1 + shares],
    )
    bands_ref, sums_ref, matrix_ref, whole_ref = refs[1 + shares :]
    me = lax.axis_index("seq")
    channels, share = piece_refs[0].shape
    samples = index_ref.shape[-1]
    plane_size = grid_side * grid_side
    band_rows = row_span + 1
    band = band_rows * grid_side
    stride = row_span * grid_side
    bands = (grid_side - 1) // row_span
    rays = tile // STEPS
    whole_rays = target_ref.shape[1]

    def column(row_ref):
        extent = row_ref.shape[1]
        on_diagonal = lax.broadcasted_iota(jnp.int32, (extent, extent), 0) == lax.broadcasted_iota(
            jnp.int32, (extent, extent), 1
        )
        return jnp.sum(jnp.where(on_diagonal, row_ref[...], 0.0), axis=1, keepdims=True)

    bias1, bias2, bias3 = column(b1_ref), column(b2_ref), column(b3_ref)
    earlier = lax.broadcasted_iota(jnp.int32, (STEPS, STEPS), 0)
    later = lax.broadcasted_iota(jnp.int32, (STEPS, STEPS), 1)
    sum_before = jnp.where(earlier < later, 1.0, 0.0)
    sum_behind = jnp.where(earlier > later, 1.0, 0.0)

    for k in range(shares):
        whole_ref[me ^ k] = piece_refs[k][...]
    whole_planes = jnp.concatenate([whole_ref[i] for i in range(shares)], axis=1)
    for plane in range(PLANES):
        for q in range(bands):
            start = plane * plane_size + q * stride
            lead = start % LANES
            extent = band + (LANES if lead else 0)
            piece = whole_planes[:, start - lead : start - lead + extent]
            if lead:
                piece = shifted_left(piece.astype(F32), lead).astype(BF16)
            bands_ref[plane, q * channels : (q + 1) * channels, :] = piece[:, :band]

    def interpolate(part):
        part_samples = slice(part * tile, (part + 1) * tile)
        index = index_ref[:, part_samples]
        weights = weight_ref[:, part_samples].astype(F32)
        features = jnp.zeros((channels, tile), F32)
        x_ids = lax.broadcasted_iota(jnp.int32, (grid_side, tile), 0)
        band_ids = []
        for plane in range(PLANES):
            in_plane = (index >= plane * plane_size) & (index < (plane + 1) * plane_size)
            base = jnp.min(jnp.where(in_plane, index, PLANES * plane_size), axis=0, keepdims=True)
            picked = [
                jnp.sum(jnp.where(index == base + shift, weights, 0.0), axis=0, keepdims=True)
                for shift in (0, 1, grid_side, grid_side + 1)
            ]
            local = base - plane * plane_size
            first_row = local // grid_side
            first_x = local - first_row * grid_side
            band_id = first_row // row_span
            band_row = first_row - band_id * row_span
            band_ids.append(band_id)
            at_first = x_ids == first_x
            at_second = x_ids == first_x + 1
            upper = jnp.where(at_first, picked[0], jnp.where(at_second, picked[1], 0.0))
            lower = jnp.where(at_first, picked[2], jnp.where(at_second, picked[3], 0.0))
            upper, lower = upper.astype(BF16), lower.astype(BF16)
            marks = [jnp.where(band_row == r, 1.0, 0.0).astype(BF16) for r in range(row_span)]
            for r in range(band_rows):
                block = upper * marks[r] if r < row_span else None
                if r > 0:
                    below = lower * marks[r - 1]
                    block = below if block is None else block + below
                matrix_ref[plane, r * grid_side : (r + 1) * grid_side, part_samples] = block
            products = jnp.dot(
                bands_ref[plane], matrix_ref[plane, :, part_samples], preferred_element_type=F32
            )
            for q in range(bands):
                features = features + jnp.where(
                    band_id == q, products[q * channels : (q + 1) * channels, :], 0.0
                )
        return features.astype(BF16), band_ids

    def shade(part, features):
        pre1 = jnp.dot(w1_ref[...], features, preferred_element_type=F32) + bias1
        gate1 = jax.nn.sigmoid(pre1)
        hidden1 = (pre1 * gate1).astype(BF16)
        pre2 = jnp.dot(w2_ref[...], hidden1, preferred_element_type=F32) + bias2
        gate2 = jax.nn.sigmoid(pre2)
        hidden2 = (pre2 * gate2).astype(BF16)
        decoded = jnp.dot(w3_ref[...], hidden2, preferred_element_type=F32) + bias3

        def by_ray(row):
            return jnp.concatenate(
                [decoded[row : row + 1, i * STEPS : (i + 1) * STEPS] for i in range(rays)], axis=0
            )

        def along_lanes(by_rays):
            return jnp.concatenate([by_rays[i : i + 1, :] for i in range(rays)], axis=1)

        raw_density = by_ray(0)
        density = jnp.maximum(raw_density, 0.0) + jnp.log1p(jnp.exp(-jnp.abs(raw_density)))
        optical = density * DEPTH_STEP
        before = jnp.dot(
            optical, sum_before, preferred_element_type=F32, precision=lax.Precision.HIGHEST
        )
        through = jnp.exp(-before)
        passing = jnp.exp(-optical)
        ray_weight = through * (1.0 - passing)
        own_ray = lax.broadcasted_iota(jnp.int32, (rays, whole_rays), 1) == (
            part * rays + lax.broadcasted_iota(jnp.int32, (rays, whole_rays), 0)
        )
        weight_slope = jnp.zeros((rays, STEPS), F32)
        color_rows = []
        decoded_slopes = []
        for channel in range(3):
            albedo = jax.nn.sigmoid(by_ray(1 + channel))
            color = jnp.sum(ray_weight * albedo, axis=1, keepdims=True)
            color_rows.append(jnp.sum(jnp.where(own_ray, color, 0.0), axis=0, keepdims=True))
            target = target_ref[channel : channel + 1, :]
            residual = color - jnp.sum(jnp.where(own_ray, target, 0.0), axis=1, keepdims=True)
            weight_slope = weight_slope + residual * albedo
            decoded_slopes.append(along_lanes(residual * ray_weight * albedo * (1.0 - albedo)))
        behind = jnp.dot(
            weight_slope * ray_weight,
            sum_behind,
            preferred_element_type=F32,
            precision=lax.Precision.HIGHEST,
        )
        optical_slope = weight_slope * through * passing - behind
        density_slope = optical_slope * DEPTH_STEP * jax.nn.sigmoid(raw_density)
        decoded_slope = jnp.concatenate([along_lanes(density_slope)] + decoded_slopes, axis=0)
        hidden2_slope = contract(w3_ref[...], decoded_slope.astype(BF16), 0, 0).astype(BF16)
        pre2_slope = hidden2_slope.astype(F32) * (gate2 * (1.0 + pre2 * (1.0 - gate2)))
        hidden1_slope = contract(w2_ref[...], pre2_slope.astype(BF16), 0, 0).astype(BF16)
        pre1_slope = hidden1_slope.astype(F32) * (gate1 * (1.0 + pre1 * (1.0 - gate1)))
        slope = contract(w1_ref[...], pre1_slope.astype(BF16), 0, 0).astype(BF16)
        return jnp.concatenate(color_rows, axis=0), slope

    def scatter(part, slope, band_ids):
        part_samples = slice(part * tile, (part + 1) * tile)
        for plane in range(PLANES):
            spread = jnp.concatenate(
                [
                    slope * jnp.where(band_ids[plane] == q, 1.0, 0.0).astype(BF16)
                    for q in range(bands)
                ],
                axis=0,
            )
            share_sum = contract(spread, matrix_ref[plane, :, part_samples], 1, 1)
            if part == 0:
                sums_ref[plane] = share_sum
            else:
                sums_ref[plane] += share_sum

    colors = jnp.zeros(colors_ref.shape, F32)
    held = None
    for part in range(samples // tile):
        features, band_ids = interpolate(part)
        if held is not None:
            scatter(*held)
        part_colors, slope = shade(part, features)
        colors = colors + part_colors
        held = (part, slope, band_ids)
    scatter(*held)
    colors_ref[...] = colors

    joined = []
    for plane in range(PLANES):
        rows = []
        for kind in range(2):
            parts, reached = [], 0
            for q in range(kind, bands, 2):
                start = q * stride
                lead = start % LANES
                piece = sums_ref[plane, q * channels : (q + 1) * channels, :]
                if lead:
                    piece = jnp.concatenate([piece, jnp.zeros((channels, LANES), F32)], axis=1)
                    piece = pltpu.roll(piece, lead, 1)
                if start - lead > reached:
                    parts.append(jnp.zeros((channels, start - lead - reached), F32))
                parts.append(piece)
                reached = start - lead + piece.shape[1]
            if plane_size > reached:
                parts.append(jnp.zeros((channels, plane_size - reached), F32))
            rows.append(jnp.concatenate(parts, axis=1))
        joined.append((rows[0] + rows[1]).astype(BF16))
    joined = jnp.concatenate(joined, axis=1)
    for i in range(shares):
        whole_ref[i] = joined[:, i * share : (i + 1) * share]
    for k in range(0, shares, 2):
        even_refs[k // 2][...] = whole_ref[me ^ k]
        odd_refs[k // 2][...] = whole_ref[me ^ (k + 1)]


def render_call(pieces, index, weights, target, w1, b1, w2, b2, w3, b3):
    shares = len(pieces)
    channels, share = pieces[0].shape
    samples = index.shape[-1]
    grid_side = math.isqrt(shares * share // PLANES)
    row_span = next(span for span in range(7, 0, -1) if (grid_side - 1) % span == 0)
    bands = (grid_side - 1) // row_span
    band = (row_span + 1) * grid_side
    tile = math.gcd(samples // STEPS, TILE_RAYS) * STEPS
    row = lambda array: array.reshape(1, -1)
    colors, *grads = pl.pallas_call(
        functools.partial(render_kernel, grid_side, row_span, shares, tile),
        out_shape=[
            jax.ShapeDtypeStruct(target.shape, F32),
            *[jax.ShapeDtypeStruct((channels, share), BF16)] * shares,
        ],
        scratch_shapes=[
            pltpu.VMEM((PLANES, bands * channels, band), BF16),
            pltpu.VMEM((PLANES, bands * channels, band), F32),
            pltpu.VMEM((PLANES, band, samples), BF16),
            pltpu.VMEM((shares, channels, share), BF16),
        ],
        compiler_params=params(),
        name="render",
    )(*pieces, index, weights, target, w1, row(b1), w2, row(b2), w3, row(b3))
    return colors, grads[: shares // 2], grads[shares // 2 :]


def weight_grad_kernel(count, *refs):
    part_refs, (plane_in_ref, even_ref, odd_ref, grad_ref, chunk_ref) = refs[:count], refs[count:]
    me = lax.axis_index("seq")
    grad = part_refs[0][...].astype(F32)
    for ref in part_refs[1:]:
        grad = grad + ref[...].astype(F32)
    grad = grad.astype(BF16)
    grad_ref[...] = grad
    total = jnp.dot(grad, plane_in_ref[...], preferred_element_type=F32)
    shares, _, columns = chunk_ref.shape
    for i in range(shares):
        chunk_ref[i] = total[:, i * columns : (i + 1) * columns]
    for j in range(shares // 2):
        even_ref[j] = chunk_ref[me ^ (2 * j)]
        odd_ref[j] = chunk_ref[me ^ (2 * j + 1)]


def weight_grad_call(parts, plane_in, shares):
    rows, width = plane_in.shape
    channels = parts[0].shape[0]
    columns = width // shares
    chunks = (shares // 2, channels, columns)
    return pl.pallas_call(
        functools.partial(weight_grad_kernel, len(parts)),
        out_shape=[
            jax.ShapeDtypeStruct(chunks, F32),
            jax.ShapeDtypeStruct(chunks, F32),
            jax.ShapeDtypeStruct((channels, rows), BF16),
        ],
        scratch_shapes=[pltpu.VMEM((shares, channels, columns), F32)],
        compiler_params=pltpu.CompilerParams(vmem_limit_bytes=VMEM_BYTES),
        name="weight_grad",
    )(*parts, plane_in)


def token_grad_kernel(grad_ref, w_plane_ref, token_grad_ref):
    token_grad_ref[...] = contract(grad_ref[...], w_plane_ref[...], 0, 0).astype(BF16)


def token_grad_call(grad, w_plane_t):
    channels, rows = grad.shape
    width = w_plane_t.shape[1]
    tile = math.gcd(rows, 384)
    return pl.pallas_call(
        token_grad_kernel,
        grid=(rows // tile,),
        in_specs=[
            pl.BlockSpec((channels, tile), lambda step: (0, step)),
            whole(w_plane_t.shape),
        ],
        out_specs=pl.BlockSpec((tile, width), lambda step: (step, 0)),
        out_shape=jax.ShapeDtypeStruct((rows, width), BF16),
        cost_estimate=estimate(2 * rows * width * channels, 2 * rows * width),
        compiler_params=params(16 * MIB),
        name="token_grad",
    )(grad, w_plane_t)


def join_kernel(count, *refs):
    chunk_refs, (out_ref, chunks_ref) = refs[:count], refs[count:]
    me = lax.axis_index("seq")
    columns = chunk_refs[0].shape[1]
    for k in range(count):
        chunks_ref[me ^ k] = chunk_refs[k][...]
    for i in range(count):
        out_ref[:, i * columns : (i + 1) * columns] = chunks_ref[i]


def join_call(chunks):
    channels, columns = chunks[0].shape
    return pl.pallas_call(
        functools.partial(join_kernel, len(chunks)),
        out_shape=jax.ShapeDtypeStruct((channels, columns * len(chunks)), F32),
        scratch_shapes=[pltpu.VMEM((len(chunks), channels, columns), F32)],
        name="join_weight_grad",
    )(*chunks)


def body(
    tokens,
    image_tokens,
    norm_gain,
    w_query,
    w_key,
    w_value,
    w_out,
    w_plane,
    dec_w1,
    dec_b1,
    dec_w2,
    dec_b2,
    dec_w3,
    dec_b3,
    corner_idx,
    corner_wts,
    target_color,
):
    own_tokens = tokens[0]
    head_dim = own_tokens.shape[1] // HEADS
    query_scale = math.log2(math.e) / math.sqrt(head_dim)
    shares = lax.axis_size("seq")
    far_images = from_chips(image_tokens[0])
    images = with_other_core([image_tokens[0]])
    queries = query_call(own_tokens, w_query, query_scale)
    far_images, queries = lax.optimization_barrier((far_images, queries))
    images = images + with_other_core(far_images)
    w_plane_t = w_plane.T
    plane_in, planes = attend_call(
        images, w_key, w_value, own_tokens, queries, w_out, norm_gain, w_plane_t, head_dim
    )
    colors, kept, passed = render_call(
        gather_scene(planes),
        corner_idx[0],
        corner_wts[0],
        target_color[0],
        dec_w1,
        dec_b1,
        dec_w2,
        dec_b2,
        dec_w3,
        dec_b3,
    )
    parts = []
    for j in reversed(range(shares // 2)):
        pair = (kept[j].astype(F32) + swap(passed[j], "seq", 1).astype(F32)).astype(BF16)
        parts.append(swap(pair, "seq", 2 * j) if j else pair)
    kept, passed, grad = weight_grad_call(parts, plane_in, shares)
    pairs = kept + swap(passed, "seq", 1)
    chunk = pairs[0]
    for j in range(1, shares // 2):
        chunk = chunk + swap(pairs[j], "seq", 2 * j)
    others = [swap(chunk, "dp", k) for k in range(1, lax.axis_size("dp"))]
    token_grad = token_grad_call(grad, w_plane_t)
    others, token_grad = lax.optimization_barrier((others, token_grad))
    scenes = sum(others, chunk)
    weight_grad = join_call(gather_scene(scenes)).T
    return (colors[None], token_grad[None], weight_grad)


def solution(mesh):
    in_specs = (
        P("dp", "seq", None),
        P("dp", "seq", None),
        P(),
        P(),
        P(),
        P(),
        P(),
        P(),
        P(),
        P(),
        P(),
        P(),
        P(),
        P(),
        P("dp", None, "seq"),
        P("dp", None, "seq"),
        P("dp", None, "seq"),
    )
    out_specs = (P("dp", None, "seq"), P("dp", "seq", None), P())
    return jax.shard_map(body, mesh=mesh, in_specs=in_specs, out_specs=out_specs, check_vma=False)
```

```python
import functools
import math

import jax
import jax.numpy as jnp
from jax import lax
from jax.experimental import pallas as pl
from jax.experimental.pallas import tpu as pltpu
from jax.sharding import PartitionSpec as P

HEADS = 16
STEPS = 128
PLANES = 3
LANES = 128
TILE_RAYS = 32
TOGETHER = 4

NORM_EPS = 1e-05
DEPTH_STEP = 0.02
MIB = 1024 * 1024
VMEM_BYTES = 56 * MIB

F32 = jnp.float32
BF16 = jnp.bfloat16


def contract(left, right, left_dim, right_dim, out_type=F32, precision=None):
    return lax.dot_general(
        left,
        right,
        (((left_dim,), (right_dim,)), ((), ())),
        preferred_element_type=out_type,
        precision=precision,
    )


def plain_norm(inputs):
    row_mean = jnp.mean(inputs, axis=-1, keepdims=True)
    centred = inputs - row_mean
    row_var = jnp.mean(centred * centred, axis=-1, keepdims=True)
    return centred * lax.rsqrt(row_var + NORM_EPS)


def params(vmem_bytes=VMEM_BYTES):
    return pltpu.CompilerParams(vmem_limit_bytes=vmem_bytes)


def swap(array, axis, distance):
    pairs = [(i, i ^ distance) for i in range(lax.axis_size(axis))]
    return lax.ppermute(array, axis, pairs)


def from_chips(piece):
    return [swap(piece, "seq", k) for k in range(2, lax.axis_size("seq"), 2)]


def with_other_core(pieces):
    return [each for piece in pieces for each in (piece, swap(piece, "seq", 1))]


def gather_scene(piece):
    return with_other_core([piece]) + with_other_core(from_chips(piece))


def whole(shape):
    return pl.BlockSpec(shape, lambda step: (0,) * len(shape), pipeline_mode=pl.Buffered(1))


def kept(shape):
    return pl.BlockSpec(shape, lambda step: (0,) * len(shape))


def estimate(flops, bytes_accessed):
    return pl.CostEstimate(flops=flops, bytes_accessed=bytes_accessed, transcendentals=0)


def query_kernel(query_scale, tokens_ref, w_query_ref, queries_ref):
    normed = plain_norm(tokens_ref[...].astype(F32)).astype(BF16)
    queries = jnp.dot(normed, w_query_ref[...], preferred_element_type=F32)
    queries_ref[...] = (queries * query_scale).astype(BF16)


def query_call(tokens, w_query, query_scale):
    rows, width = tokens.shape
    tile = math.gcd(rows, 512)
    return pl.pallas_call(
        functools.partial(query_kernel, query_scale),
        grid=(rows // tile,),
        in_specs=[pl.BlockSpec((tile, width), lambda step: (step, 0)), whole(w_query.shape)],
        out_specs=pl.BlockSpec((tile, width), lambda step: (step, 0)),
        out_shape=jax.ShapeDtypeStruct((rows, width), BF16),
        cost_estimate=estimate(2 * rows * width * width, 4 * rows * width),
        compiler_params=params(32 * MIB),
        name="queries",
    )(tokens, w_query)


def attend_kernel(head_dim, shares, *refs):
    image_refs, refs = refs[:shares], refs[shares:]
    w_key_ref, w_value_ref, tokens_ref, queries_ref, w_out_ref, gain_ref, w_plane_ref = refs[:7]
    plane_in_ref, planes_ref, keys_ref, values_ref, attended_ref = refs[7:]
    rows, width = tokens_ref.shape
    groups = width // LANES

    @pl.when(pl.program_id(0) == 0)
    def project_images():
        images = jnp.concatenate([ref[...] for ref in image_refs], axis=0)
        keys = jnp.dot(images, w_key_ref[...], preferred_element_type=F32).astype(BF16)
        keys_ref[...] = keys.T
        values = jnp.dot(images, w_value_ref[...], preferred_element_type=F32).astype(BF16)
        ones = jnp.ones((values.shape[0], LANES), BF16)
        for group in range(groups):
            values_ref[group, :, :LANES] = values[:, group * LANES : (group + 1) * LANES]
            values_ref[group, :, LANES:] = ones

    lane_ids = lax.broadcasted_iota(jnp.int32, (rows, LANES), 1)
    together = math.gcd(groups, TOGETHER)
    heads = [(group, low) for group in range(together) for low in range(0, LANES, head_dim)]

    def own_lanes(low):
        return (lane_ids >= low) & (lane_ids < low + head_dim)

    def group_step(step, _):
        def columns(group):
            return pl.ds(pl.multiple_of((step * together + group) * LANES, LANES), LANES)

        def head_scores(head):
            group, low = heads[head]
            group_queries = queries_ref[:, columns(group)]
            head_queries = jnp.where(own_lanes(low), group_queries, jnp.zeros_like(group_queries))
            return jnp.dot(
                head_queries, keys_ref[columns(group), :], preferred_element_type=F32
            )

        upcoming = head_scores(0)
        joined = None
        for head, (group, low) in enumerate(heads):
            scores = upcoming
            if head + 1 < len(heads):
                upcoming = head_scores(head + 1)
            row_max = jnp.max(scores, axis=1, keepdims=True)
            probs = jnp.exp2(scores - row_max).astype(BF16)
            sums = jnp.dot(
                probs, values_ref[step * together + group], preferred_element_type=F32
            )
            head_out = sums[:, :LANES] / sums[:, LANES:]
            joined = head_out if low == 0 else jnp.where(own_lanes(low), head_out, joined)
            if low + head_dim == LANES:
                attended_ref[:, columns(group)] = joined.astype(BF16)
        return 0

    lax.fori_loop(0, groups // together, group_step, 0)
    mixed = (
        tokens_ref[...].astype(F32)
        + jnp.dot(attended_ref[...], w_out_ref[...], preferred_element_type=F32)
    ).astype(BF16)
    plane_in = (plain_norm(mixed.astype(F32)) * gain_ref[...]).astype(BF16)
    plane_in_ref[...] = plane_in
    planes_ref[...] = contract(w_plane_ref[...], plane_in, 1, 1).astype(BF16)


def attend_call(images, w_key, w_value, tokens, queries, w_out, norm_gain, w_plane_t, head_dim):
    rows, width = tokens.shape
    channels = w_plane_t.shape[0]
    image_rows = sum(piece.shape[0] for piece in images)
    tile = math.gcd(rows, 768)
    row_block = pl.BlockSpec((tile, width), lambda step: (step, 0))
    return pl.pallas_call(
        functools.partial(attend_kernel, head_dim, len(images)),
        grid=(rows // tile,),
        in_specs=[
            *[whole(piece.shape) for piece in images],
            whole(w_key.shape),
            whole(w_value.shape),
            row_block,
            row_block,
            whole(w_out.shape),
            whole((1, width)),
            whole(w_plane_t.shape),
        ],
        out_specs=[row_block, pl.BlockSpec((channels, tile), lambda step: (0, step))],
        out_shape=[
            jax.ShapeDtypeStruct((rows, width), BF16),
            jax.ShapeDtypeStruct((channels, rows), BF16),
        ],
        scratch_shapes=[
            pltpu.VMEM((width, image_rows), BF16),
            pltpu.VMEM((width // LANES, image_rows, 2 * LANES), BF16),
            pltpu.VMEM((tile, width), BF16),
        ],
        cost_estimate=estimate(4 * rows * width * (image_rows + width // 2), 2 * rows * width),
        compiler_params=params(),
        name="attention_planes",
    )(*images, w_key, w_value, tokens, queries, w_out, norm_gain.reshape(1, width), w_plane_t)


def corners_kernel(grid_side, row_span, index_ref, weight_ref, table_ref):
    index = index_ref[...]
    weights = weight_ref[...].astype(F32)
    plane_size = grid_side * grid_side
    for plane in range(PLANES):
        in_plane = (index >= plane * plane_size) & (index < (plane + 1) * plane_size)
        base = jnp.min(jnp.where(in_plane, index, PLANES * plane_size), axis=0, keepdims=True)
        local = base - plane * plane_size
        first_row = local // grid_side
        band_id = first_row // row_span
        places = [band_id, first_row - band_id * row_span, local - first_row * grid_side]
        picked = [
            jnp.sum(jnp.where(index == base + shift, weights, 0.0), axis=0, keepdims=True)
            for shift in (0, 1, grid_side, grid_side + 1)
        ]
        rows = [place.astype(F32) for place in places] + picked + [jnp.zeros_like(picked[0])]
        table_ref[plane] = jnp.concatenate(rows, axis=0)


def corners_call(index, weights, tokens):
    samples = index.shape[1]
    grid_side = math.isqrt(tokens // PLANES)
    return pl.pallas_call(
        functools.partial(corners_kernel, grid_side, band_span(grid_side)),
        out_shape=jax.ShapeDtypeStruct((PLANES, 8, samples), F32),
        cost_estimate=estimate(1000 * samples, 100 * samples),
        compiler_params=params(16 * MIB),
        name="corners",
    )(index, weights)


def band_span(grid_side):
    return next(span for span in range(7, 0, -1) if (grid_side - 1) % span == 0)


def shifted_left(block, lanes):
    return pltpu.roll(block, block.shape[1] - lanes, 1) if lanes else block


def render_kernel(grid_side, row_span, shares, tile, *refs):
    piece_refs, refs = refs[:shares], refs[shares:]
    (table_ref, target_ref, w1_ref, b1_ref, w2_ref, b2_ref, w3_ref, b3_ref), refs = (
        refs[:8],
        refs[8:],
    )
    colors_ref, even_refs, odd_refs = (
        refs[0],
        refs[1 : 1 + shares // 2],
        refs[1 + shares // 2 : 1 + shares],
    )
    bands_ref, sums_ref, matrix_ref, whole_ref, slope_ref = refs[1 + shares :]
    me = lax.axis_index("seq")
    channels, share = piece_refs[0].shape
    samples = table_ref.shape[-1]
    plane_size = grid_side * grid_side
    band_rows = row_span + 1
    band = band_rows * grid_side
    stride = row_span * grid_side
    bands = (grid_side - 1) // row_span
    rays = tile // STEPS
    whole_rays = target_ref.shape[1]

    def column(row_ref):
        extent = row_ref.shape[1]
        on_diagonal = lax.broadcasted_iota(jnp.int32, (extent, extent), 0) == lax.broadcasted_iota(
            jnp.int32, (extent, extent), 1
        )
        return jnp.sum(jnp.where(on_diagonal, row_ref[...], 0.0), axis=1, keepdims=True)

    bias1, bias2, bias3 = column(b1_ref), column(b2_ref), column(b3_ref)
    earlier = lax.broadcasted_iota(jnp.int32, (STEPS, STEPS), 0)
    later = lax.broadcasted_iota(jnp.int32, (STEPS, STEPS), 1)
    sum_before = jnp.where(earlier < later, 1.0, 0.0)
    sum_behind = jnp.where(earlier > later, 1.0, 0.0)

    for k in range(shares):
        whole_ref[me ^ k] = piece_refs[k][...]
    whole_planes = jnp.concatenate([whole_ref[i] for i in range(shares)], axis=1)
    for plane in range(PLANES):
        for q in range(bands):
            start = plane * plane_size + q * stride
            lead = start % LANES
            extent = band + (LANES if lead else 0)
            piece = whole_planes[:, start - lead : start - lead + extent]
            if lead:
                piece = shifted_left(piece.astype(F32), lead).astype(BF16)
            bands_ref[plane, q * channels : (q + 1) * channels, :] = piece[:, :band]

    def interpolate(part):
        part_samples = pl.ds(pl.multiple_of(part * tile, tile), tile)
        features = jnp.zeros((channels, tile), F32)
        x_ids = lax.broadcasted_iota(jnp.int32, (grid_side, tile), 0).astype(F32)
        for plane in range(PLANES):
            band_id, band_row, first_x, *picked = (
                table_ref[plane, row : row + 1, part_samples] for row in range(7)
            )
            at_first = x_ids == first_x
            at_second = x_ids == first_x + 1.0
            upper = jnp.where(at_first, picked[0], jnp.where(at_second, picked[1], 0.0))
            lower = jnp.where(at_first, picked[2], jnp.where(at_second, picked[3], 0.0))
            upper, lower = upper.astype(BF16), lower.astype(BF16)
            marks = [jnp.where(band_row == r, 1.0, 0.0).astype(BF16) for r in range(row_span)]
            for r in range(band_rows):
                block = upper * marks[r] if r < row_span else None
                if r > 0:
                    below = lower * marks[r - 1]
                    block = below if block is None else block + below
                matrix_ref[plane, r * grid_side : (r + 1) * grid_side, part_samples] = block
            products = jnp.dot(
                bands_ref[plane], matrix_ref[plane, :, part_samples], preferred_element_type=F32
            )
            for q in range(bands):
                features = features + jnp.where(
                    band_id == q, products[q * channels : (q + 1) * channels, :], 0.0
                )
        return features.astype(BF16)

    def shade(part, features):
        pre1 = jnp.dot(w1_ref[...], features, preferred_element_type=F32) + bias1
        gate1 = jax.nn.sigmoid(pre1)
        hidden1 = (pre1 * gate1).astype(BF16)
        pre2 = jnp.dot(w2_ref[...], hidden1, preferred_element_type=F32) + bias2
        gate2 = jax.nn.sigmoid(pre2)
        hidden2 = (pre2 * gate2).astype(BF16)
        decoded = jnp.dot(w3_ref[...], hidden2, preferred_element_type=F32) + bias3

        def by_ray(row):
            return jnp.concatenate(
                [decoded[row : row + 1, i * STEPS : (i + 1) * STEPS] for i in range(rays)], axis=0
            )

        def along_lanes(by_rays):
            return jnp.concatenate([by_rays[i : i + 1, :] for i in range(rays)], axis=1)

        raw_density = by_ray(0)
        density = jnp.maximum(raw_density, 0.0) + jnp.log1p(jnp.exp(-jnp.abs(raw_density)))
        optical = density * DEPTH_STEP
        before = jnp.dot(
            optical, sum_before, preferred_element_type=F32, precision=lax.Precision.HIGHEST
        )
        through = jnp.exp(-before)
        passing = jnp.exp(-optical)
        ray_weight = through * (1.0 - passing)
        own_ray = lax.broadcasted_iota(jnp.int32, (rays, whole_rays), 1) == (
            part * rays + lax.broadcasted_iota(jnp.int32, (rays, whole_rays), 0)
        )
        weight_slope = jnp.zeros((rays, STEPS), F32)
        color_rows = []
        decoded_slopes = []
        for channel in range(3):
            albedo = jax.nn.sigmoid(by_ray(1 + channel))
            color = jnp.sum(ray_weight * albedo, axis=1, keepdims=True)
            color_rows.append(jnp.sum(jnp.where(own_ray, color, 0.0), axis=0, keepdims=True))
            target = target_ref[channel : channel + 1, :]
            residual = color - jnp.sum(jnp.where(own_ray, target, 0.0), axis=1, keepdims=True)
            weight_slope = weight_slope + residual * albedo
            decoded_slopes.append(along_lanes(residual * ray_weight * albedo * (1.0 - albedo)))
        behind = jnp.dot(
            weight_slope * ray_weight,
            sum_behind,
            preferred_element_type=F32,
            precision=lax.Precision.HIGHEST,
        )
        optical_slope = weight_slope * through * passing - behind
        density_slope = optical_slope * DEPTH_STEP * jax.nn.sigmoid(raw_density)
        decoded_slope = jnp.concatenate([along_lanes(density_slope)] + decoded_slopes, axis=0)
        hidden2_slope = contract(w3_ref[...], decoded_slope.astype(BF16), 0, 0).astype(BF16)
        pre2_slope = hidden2_slope.astype(F32) * (gate2 * (1.0 + pre2 * (1.0 - gate2)))
        hidden1_slope = contract(w2_ref[...], pre2_slope.astype(BF16), 0, 0).astype(BF16)
        pre1_slope = hidden1_slope.astype(F32) * (gate1 * (1.0 + pre1 * (1.0 - gate1)))
        slope = contract(w1_ref[...], pre1_slope.astype(BF16), 0, 0).astype(BF16)
        return jnp.concatenate(color_rows, axis=0), slope

    colors_ref[...] = jnp.zeros(colors_ref.shape, F32)

    def render_part(part, _):
        colors, slope = shade(part, interpolate(part))
        colors_ref[...] += colors
        slope_ref[:, pl.ds(pl.multiple_of(part * tile, tile), tile)] = slope
        return 0

    lax.fori_loop(0, samples // tile, render_part, 0)

    def scatter(plane, _):
        slope = slope_ref[...]
        band_id = table_ref[plane, 0:1, :]
        spread = jnp.concatenate(
            [slope * jnp.where(band_id == q, 1.0, 0.0).astype(BF16) for q in range(bands)], axis=0
        )
        sums_ref[plane] = contract(spread, matrix_ref[plane], 1, 1)
        return 0

    lax.fori_loop(0, PLANES, scatter, 0)

    joined = []
    for plane in range(PLANES):
        rows = []
        for kind in range(2):
            parts, reached = [], 0
            for q in range(kind, bands, 2):
                start = q * stride
                lead = start % LANES
                piece = sums_ref[plane, q * channels : (q + 1) * channels, :]
                if lead:
                    piece = jnp.concatenate([piece, jnp.zeros((channels, LANES), F32)], axis=1)
                    piece = pltpu.roll(piece, lead, 1)
                if start - lead > reached:
                    parts.append(jnp.zeros((channels, start - lead - reached), F32))
                parts.append(piece)
                reached = start - lead + piece.shape[1]
            if plane_size > reached:
                parts.append(jnp.zeros((channels, plane_size - reached), F32))
            rows.append(jnp.concatenate(parts, axis=1))
        joined.append((rows[0] + rows[1]).astype(BF16))
    joined = jnp.concatenate(joined, axis=1)
    for i in range(shares):
        whole_ref[i] = joined[:, i * share : (i + 1) * share]
    for k in range(0, shares, 2):
        even_refs[k // 2][...] = whole_ref[me ^ k]
        odd_refs[k // 2][...] = whole_ref[me ^ (k + 1)]


def render_call(pieces, table, target, w1, b1, w2, b2, w3, b3):
    shares = len(pieces)
    channels, share = pieces[0].shape
    samples = table.shape[-1]
    grid_side = math.isqrt(shares * share // PLANES)
    row_span = band_span(grid_side)
    bands = (grid_side - 1) // row_span
    band = (row_span + 1) * grid_side
    tile = math.gcd(samples // STEPS, TILE_RAYS) * STEPS
    row = lambda array: array.reshape(1, -1)
    colors, *grads = pl.pallas_call(
        functools.partial(render_kernel, grid_side, row_span, shares, tile),
        out_shape=[
            jax.ShapeDtypeStruct(target.shape, F32),
            *[jax.ShapeDtypeStruct((channels, share), BF16)] * shares,
        ],
        scratch_shapes=[
            pltpu.VMEM((PLANES, bands * channels, band), BF16),
            pltpu.VMEM((PLANES, bands * channels, band), F32),
            pltpu.VMEM((PLANES, band, samples), BF16),
            pltpu.VMEM((shares, channels, share), BF16),
            pltpu.VMEM((channels, samples), BF16),
        ],
        compiler_params=params(),
        name="render",
    )(*pieces, table, target, w1, row(b1), w2, row(b2), w3, row(b3))
    return colors, grads[: shares // 2], grads[shares // 2 :]


def weight_grad_kernel(count, *refs):
    part_refs, (plane_in_ref, even_ref, odd_ref, grad_ref, chunk_ref) = refs[:count], refs[count:]
    me = lax.axis_index("seq")
    grad = part_refs[0][...].astype(F32)
    for ref in part_refs[1:]:
        grad = grad + ref[...].astype(F32)
    grad = grad.astype(BF16)
    grad_ref[...] = grad
    total = jnp.dot(grad, plane_in_ref[...], preferred_element_type=F32)
    shares, _, columns = chunk_ref.shape
    for i in range(shares):
        chunk_ref[i] = total[:, i * columns : (i + 1) * columns]
    for j in range(shares // 2):
        even_ref[j] = chunk_ref[me ^ (2 * j)]
        odd_ref[j] = chunk_ref[me ^ (2 * j + 1)]


def weight_grad_call(parts, plane_in, shares):
    rows, width = plane_in.shape
    channels = parts[0].shape[0]
    columns = width // shares
    chunks = (shares // 2, channels, columns)
    return pl.pallas_call(
        functools.partial(weight_grad_kernel, len(parts)),
        out_shape=[
            jax.ShapeDtypeStruct(chunks, F32),
            jax.ShapeDtypeStruct(chunks, F32),
            jax.ShapeDtypeStruct((channels, rows), BF16),
        ],
        scratch_shapes=[pltpu.VMEM((shares, channels, columns), F32)],
        compiler_params=pltpu.CompilerParams(vmem_limit_bytes=VMEM_BYTES),
        name="weight_grad",
    )(*parts, plane_in)


def token_grad_kernel(grad_ref, w_plane_ref, token_grad_ref):
    token_grad_ref[...] = contract(grad_ref[...], w_plane_ref[...], 0, 0).astype(BF16)


def token_grad_call(grad, w_plane_t):
    channels, rows = grad.shape
    width = w_plane_t.shape[1]
    tile = math.gcd(rows, 384)
    return pl.pallas_call(
        token_grad_kernel,
        grid=(rows // tile,),
        in_specs=[
            pl.BlockSpec((channels, tile), lambda step: (0, step)),
            whole(w_plane_t.shape),
        ],
        out_specs=pl.BlockSpec((tile, width), lambda step: (step, 0)),
        out_shape=jax.ShapeDtypeStruct((rows, width), BF16),
        cost_estimate=estimate(2 * rows * width * channels, 2 * rows * width),
        compiler_params=params(16 * MIB),
        name="token_grad",
    )(grad, w_plane_t)


def join_kernel(count, *refs):
    chunk_refs, (out_ref, chunks_ref) = refs[:count], refs[count:]
    me = lax.axis_index("seq")
    columns = chunk_refs[0].shape[1]
    for k in range(count):
        chunks_ref[me ^ k] = chunk_refs[k][...]
    for i in range(count):
        out_ref[:, i * columns : (i + 1) * columns] = chunks_ref[i]


def join_call(chunks):
    channels, columns = chunks[0].shape
    return pl.pallas_call(
        functools.partial(join_kernel, len(chunks)),
        out_shape=jax.ShapeDtypeStruct((channels, columns * len(chunks)), F32),
        scratch_shapes=[pltpu.VMEM((len(chunks), channels, columns), F32)],
        name="join_weight_grad",
    )(*chunks)


def body(
    tokens,
    image_tokens,
    norm_gain,
    w_query,
    w_key,
    w_value,
    w_out,
    w_plane,
    dec_w1,
    dec_b1,
    dec_w2,
    dec_b2,
    dec_w3,
    dec_b3,
    corner_idx,
    corner_wts,
    target_color,
):
    own_tokens = tokens[0]
    head_dim = own_tokens.shape[1] // HEADS
    query_scale = math.log2(math.e) / math.sqrt(head_dim)
    shares = lax.axis_size("seq")
    rows_here = own_tokens.shape[0]
    far_images = from_chips(image_tokens[0])
    images = with_other_core([image_tokens[0]])
    queries = query_call(own_tokens, w_query, query_scale)
    far_images, queries = lax.optimization_barrier((far_images, queries))
    images = images + with_other_core(far_images)
    w_plane_t = w_plane.T
    plane_in, planes = attend_call(
        images, w_key, w_value, own_tokens, queries, w_out, norm_gain, w_plane_t, head_dim
    )
    far_planes = from_chips(planes)
    planes = with_other_core([planes])
    table = corners_call(corner_idx[0], corner_wts[0], shares * rows_here)
    far_planes, table = lax.optimization_barrier((far_planes, table))
    colors, kept, passed = render_call(
        planes + with_other_core(far_planes),
        table,
        target_color[0],
        dec_w1,
        dec_b1,
        dec_w2,
        dec_b2,
        dec_w3,
        dec_b3,
    )
    parts = []
    for j in reversed(range(shares // 2)):
        pair = (kept[j].astype(F32) + swap(passed[j], "seq", 1).astype(F32)).astype(BF16)
        parts.append(swap(pair, "seq", 2 * j) if j else pair)
    kept, passed, grad = weight_grad_call(parts, plane_in, shares)
    pairs = kept + swap(passed, "seq", 1)
    chunk = pairs[0]
    for j in range(1, shares // 2):
        chunk = chunk + swap(pairs[j], "seq", 2 * j)
    others = [swap(chunk, "dp", k) for k in range(1, lax.axis_size("dp"))]
    token_grad = token_grad_call(grad, w_plane_t)
    others, token_grad = lax.optimization_barrier((others, token_grad))
    scenes = sum(others, chunk)
    weight_grad = join_call(gather_scene(scenes)).T
    return (colors[None], token_grad[None], weight_grad)


def solution(mesh):
    in_specs = (
        P("dp", "seq", None),
        P("dp", "seq", None),
        P(),
        P(),
        P(),
        P(),
        P(),
        P(),
        P(),
        P(),
        P(),
        P(),
        P(),
        P(),
        P("dp", None, "seq"),
        P("dp", None, "seq"),
        P("dp", None, "seq"),
    )
    out_specs = (P("dp", None, "seq"), P("dp", "seq", None), P())
    return jax.shard_map(body, mesh=mesh, in_specs=in_specs, out_specs=out_specs, check_vma=False)
```

```python
import functools
import math

import jax
import jax.numpy as jnp
from jax import lax
from jax.experimental import pallas as pl
from jax.experimental.pallas import tpu as pltpu
from jax.sharding import PartitionSpec as P

HEADS = 16
STEPS = 128
PLANES = 3
LANES = 128
TILE_RAYS = 32
TOGETHER = 8

NORM_EPS = 1e-05
DEPTH_STEP = 0.02
MIB = 1024 * 1024
VMEM_BYTES = 60 * MIB

F32 = jnp.float32
BF16 = jnp.bfloat16


def contract(left, right, left_dim, right_dim, out_type=F32, precision=None):
    return lax.dot_general(
        left,
        right,
        (((left_dim,), (right_dim,)), ((), ())),
        preferred_element_type=out_type,
        precision=precision,
    )


def plain_norm(inputs):
    row_mean = jnp.mean(inputs, axis=-1, keepdims=True)
    centred = inputs - row_mean
    row_var = jnp.mean(centred * centred, axis=-1, keepdims=True)
    return centred * lax.rsqrt(row_var + NORM_EPS)


def params(vmem_bytes=VMEM_BYTES):
    return pltpu.CompilerParams(vmem_limit_bytes=vmem_bytes)


def swap(array, axis, distance):
    pairs = [(i, i ^ distance) for i in range(lax.axis_size(axis))]
    return lax.ppermute(array, axis, pairs)


def from_chips(piece):
    return [swap(piece, "seq", k) for k in range(2, lax.axis_size("seq"), 2)]


def with_other_core(pieces):
    return [each for piece in pieces for each in (piece, swap(piece, "seq", 1))]


def gather_scene(piece):
    return with_other_core([piece]) + with_other_core(from_chips(piece))


def whole(shape):
    return pl.BlockSpec(shape, lambda step: (0,) * len(shape), pipeline_mode=pl.Buffered(1))


def kept(shape):
    return pl.BlockSpec(shape, lambda step: (0,) * len(shape))


def estimate(flops, bytes_accessed):
    return pl.CostEstimate(flops=flops, bytes_accessed=bytes_accessed, transcendentals=0)


def query_kernel(query_scale, tokens_ref, w_query_ref, queries_ref):
    normed = plain_norm(tokens_ref[...].astype(F32)).astype(BF16)
    queries = jnp.dot(normed, w_query_ref[...], preferred_element_type=F32)
    queries_ref[...] = (queries * query_scale).astype(BF16)


def query_call(tokens, w_query, query_scale):
    rows, width = tokens.shape
    tile = math.gcd(rows, 512)
    return pl.pallas_call(
        functools.partial(query_kernel, query_scale),
        grid=(rows // tile,),
        in_specs=[pl.BlockSpec((tile, width), lambda step: (step, 0)), whole(w_query.shape)],
        out_specs=pl.BlockSpec((tile, width), lambda step: (step, 0)),
        out_shape=jax.ShapeDtypeStruct((rows, width), BF16),
        cost_estimate=estimate(2 * rows * width * width, 4 * rows * width),
        compiler_params=params(),
        name="queries",
    )(tokens, w_query)


def attend_kernel(head_dim, shares, *refs):
    image_refs, refs = refs[:shares], refs[shares:]
    w_key_ref, w_value_ref, tokens_ref, queries_ref, w_out_ref, gain_ref, w_plane_ref = refs[:7]
    plane_in_ref, planes_ref, keys_ref, values_ref, attended_ref = refs[7:]
    rows, width = tokens_ref.shape
    groups = width // LANES

    @pl.when(pl.program_id(0) == 0)
    def project_images():
        images = jnp.concatenate([ref[...] for ref in image_refs], axis=0)
        keys = jnp.dot(images, w_key_ref[...], preferred_element_type=F32).astype(BF16)
        keys_ref[...] = keys.T
        values = jnp.dot(images, w_value_ref[...], preferred_element_type=F32).astype(BF16)
        ones = jnp.ones((values.shape[0], LANES), BF16)
        for group in range(groups):
            values_ref[group, :, :LANES] = values[:, group * LANES : (group + 1) * LANES]
            values_ref[group, :, LANES:] = ones

    lane_ids = lax.broadcasted_iota(jnp.int32, (rows, LANES), 1)
    together = math.gcd(groups, TOGETHER)
    heads = [(group, low) for group in range(together) for low in range(0, LANES, head_dim)]

    def own_lanes(low):
        return (lane_ids >= low) & (lane_ids < low + head_dim)

    def group_step(step, _):
        def columns(group):
            return pl.ds(pl.multiple_of((step * together + group) * LANES, LANES), LANES)

        def head_scores(head):
            group, low = heads[head]
            group_queries = queries_ref[:, columns(group)]
            head_queries = jnp.where(own_lanes(low), group_queries, jnp.zeros_like(group_queries))
            return jnp.dot(
                head_queries, keys_ref[columns(group), :], preferred_element_type=F32
            )

        upcoming = head_scores(0)
        joined = None
        for head, (group, low) in enumerate(heads):
            scores = upcoming
            if head + 1 < len(heads):
                upcoming = head_scores(head + 1)
            row_max = jnp.max(scores, axis=1, keepdims=True)
            probs = jnp.exp2(scores - row_max).astype(BF16)
            sums = jnp.dot(
                probs, values_ref[step * together + group], preferred_element_type=F32
            )
            head_out = sums[:, :LANES] / sums[:, LANES:]
            joined = head_out if low == 0 else jnp.where(own_lanes(low), head_out, joined)
            if low + head_dim == LANES:
                attended_ref[:, columns(group)] = joined.astype(BF16)
        return 0

    lax.fori_loop(0, groups // together, group_step, 0)
    mixed = (
        tokens_ref[...].astype(F32)
        + jnp.dot(attended_ref[...], w_out_ref[...], preferred_element_type=F32)
    ).astype(BF16)
    plane_in = (plain_norm(mixed.astype(F32)) * gain_ref[...]).astype(BF16)
    plane_in_ref[...] = plane_in
    planes_ref[...] = contract(w_plane_ref[...], plane_in, 1, 1).astype(BF16)


def attend_call(images, w_key, w_value, tokens, queries, w_out, norm_gain, w_plane_t, head_dim):
    rows, width = tokens.shape
    channels = w_plane_t.shape[0]
    image_rows = sum(piece.shape[0] for piece in images)
    tile = math.gcd(rows, 384)
    row_block = pl.BlockSpec((tile, width), lambda step: (step, 0))
    return pl.pallas_call(
        functools.partial(attend_kernel, head_dim, len(images)),
        grid=(rows // tile,),
        in_specs=[
            *[whole(piece.shape) for piece in images],
            whole(w_key.shape),
            whole(w_value.shape),
            row_block,
            row_block,
            whole(w_out.shape),
            whole((1, width)),
            whole(w_plane_t.shape),
        ],
        out_specs=[row_block, pl.BlockSpec((channels, tile), lambda step: (0, step))],
        out_shape=[
            jax.ShapeDtypeStruct((rows, width), BF16),
            jax.ShapeDtypeStruct((channels, rows), BF16),
        ],
        scratch_shapes=[
            pltpu.VMEM((width, image_rows), BF16),
            pltpu.VMEM((width // LANES, image_rows, 2 * LANES), BF16),
            pltpu.VMEM((tile, width), BF16),
        ],
        cost_estimate=estimate(4 * rows * width * (image_rows + width // 2), 2 * rows * width),
        compiler_params=params(),
        name="attention_planes",
    )(*images, w_key, w_value, tokens, queries, w_out, norm_gain.reshape(1, width), w_plane_t)


def corners_kernel(
    grid_side, row_span, index_ref, weight_ref, target_ref, table_ref, target_out_ref
):
    target_out_ref[...] = target_ref[...]
    index = index_ref[...]
    weights = weight_ref[...].astype(F32)
    plane_size = grid_side * grid_side
    for plane in range(PLANES):
        in_plane = (index >= plane * plane_size) & (index < (plane + 1) * plane_size)
        base = jnp.min(jnp.where(in_plane, index, PLANES * plane_size), axis=0, keepdims=True)
        local = base - plane * plane_size
        first_row = local // grid_side
        band_id = first_row // row_span
        places = [band_id, first_row - band_id * row_span, local - first_row * grid_side]
        picked = [
            jnp.sum(jnp.where(index == base + shift, weights, 0.0), axis=0, keepdims=True)
            for shift in (0, 1, grid_side, grid_side + 1)
        ]
        rows = [place.astype(F32) for place in places] + picked + [jnp.zeros_like(picked[0])]
        table_ref[plane] = jnp.concatenate(rows, axis=0)


def corners_call(index, weights, target, tokens):
    samples = index.shape[1]
    grid_side = math.isqrt(tokens // PLANES)
    return pl.pallas_call(
        functools.partial(corners_kernel, grid_side, band_span(grid_side)),
        out_shape=[
            jax.ShapeDtypeStruct((PLANES, 8, samples), F32),
            jax.ShapeDtypeStruct(target.shape, F32),
        ],
        cost_estimate=estimate(1000 * samples, 100 * samples),
        compiler_params=params(16 * MIB),
        name="corners",
    )(index, weights, target)


def band_span(grid_side):
    return next(span for span in range(7, 0, -1) if (grid_side - 1) % span == 0)


def shifted_left(block, lanes):
    return pltpu.roll(block, block.shape[1] - lanes, 1) if lanes else block


def render_kernel(grid_side, row_span, shares, tile, *refs):
    piece_refs, refs = refs[:shares], refs[shares:]
    (table_ref, target_ref, w1_ref, b1_ref, w2_ref, b2_ref, w3_ref, b3_ref), refs = (
        refs[:8],
        refs[8:],
    )
    colors_ref, even_refs, odd_refs = (
        refs[0],
        refs[1 : 1 + shares // 2],
        refs[1 + shares // 2 : 1 + shares],
    )
    bands_ref, sums_ref, matrix_ref, whole_ref, slope_ref = refs[1 + shares :]
    me = lax.axis_index("seq")
    channels, share = piece_refs[0].shape
    samples = table_ref.shape[-1]
    plane_size = grid_side * grid_side
    band_rows = row_span + 1
    band = band_rows * grid_side
    stride = row_span * grid_side
    bands = (grid_side - 1) // row_span
    rays = tile // STEPS
    whole_rays = target_ref.shape[1]

    def column(row_ref):
        extent = row_ref.shape[1]
        on_diagonal = lax.broadcasted_iota(jnp.int32, (extent, extent), 0) == lax.broadcasted_iota(
            jnp.int32, (extent, extent), 1
        )
        return jnp.sum(jnp.where(on_diagonal, row_ref[...], 0.0), axis=1, keepdims=True)

    bias1, bias2, bias3 = column(b1_ref), column(b2_ref), column(b3_ref)
    earlier = lax.broadcasted_iota(jnp.int32, (STEPS, STEPS), 0)
    later = lax.broadcasted_iota(jnp.int32, (STEPS, STEPS), 1)
    sum_before = jnp.where(earlier < later, 1.0, 0.0)
    sum_behind = jnp.where(earlier > later, 1.0, 0.0)

    for k in range(shares):
        whole_ref[me ^ k] = piece_refs[k][...]
    whole_planes = jnp.concatenate([whole_ref[i] for i in range(shares)], axis=1)
    for plane in range(PLANES):
        for q in range(bands):
            start = plane * plane_size + q * stride
            lead = start % LANES
            extent = band + (LANES if lead else 0)
            piece = whole_planes[:, start - lead : start - lead + extent]
            if lead:
                piece = shifted_left(piece.astype(F32), lead).astype(BF16)
            bands_ref[plane, q * channels : (q + 1) * channels, :] = piece[:, :band]

    def interpolate(part):
        part_samples = pl.ds(pl.multiple_of(part * tile, tile), tile)
        features = jnp.zeros((channels, tile), F32)
        x_ids = lax.broadcasted_iota(jnp.int32, (grid_side, tile), 0).astype(F32)
        for plane in range(PLANES):
            band_id, band_row, first_x, *picked = (
                table_ref[plane, row : row + 1, part_samples] for row in range(7)
            )
            at_first = x_ids == first_x
            at_second = x_ids == first_x + 1.0
            upper = jnp.where(at_first, picked[0], jnp.where(at_second, picked[1], 0.0))
            lower = jnp.where(at_first, picked[2], jnp.where(at_second, picked[3], 0.0))
            upper, lower = upper.astype(BF16), lower.astype(BF16)
            marks = [jnp.where(band_row == r, 1.0, 0.0).astype(BF16) for r in range(row_span)]
            for r in range(band_rows):
                block = upper * marks[r] if r < row_span else None
                if r > 0:
                    below = lower * marks[r - 1]
                    block = below if block is None else block + below
                matrix_ref[plane, r * grid_side : (r + 1) * grid_side, part_samples] = block
            products = jnp.dot(
                bands_ref[plane], matrix_ref[plane, :, part_samples], preferred_element_type=F32
            )
            for q in range(bands):
                features = features + jnp.where(
                    band_id == q, products[q * channels : (q + 1) * channels, :], 0.0
                )
        return features.astype(BF16)

    def shade(part, features):
        pre1 = jnp.dot(w1_ref[...], features, preferred_element_type=F32) + bias1
        gate1 = jax.nn.sigmoid(pre1)
        hidden1 = (pre1 * gate1).astype(BF16)
        pre2 = jnp.dot(w2_ref[...], hidden1, preferred_element_type=F32) + bias2
        gate2 = jax.nn.sigmoid(pre2)
        hidden2 = (pre2 * gate2).astype(BF16)
        decoded = jnp.dot(w3_ref[...], hidden2, preferred_element_type=F32) + bias3

        def by_ray(row):
            return jnp.concatenate(
                [decoded[row : row + 1, i * STEPS : (i + 1) * STEPS] for i in range(rays)], axis=0
            )

        def along_lanes(by_rays):
            return jnp.concatenate([by_rays[i : i + 1, :] for i in range(rays)], axis=1)

        raw_density = by_ray(0)
        density = jnp.maximum(raw_density, 0.0) + jnp.log1p(jnp.exp(-jnp.abs(raw_density)))
        optical = density * DEPTH_STEP
        before = jnp.dot(
            optical, sum_before, preferred_element_type=F32, precision=lax.Precision.HIGHEST
        )
        through = jnp.exp(-before)
        passing = jnp.exp(-optical)
        ray_weight = through * (1.0 - passing)
        own_ray = lax.broadcasted_iota(jnp.int32, (rays, whole_rays), 1) == (
            part * rays + lax.broadcasted_iota(jnp.int32, (rays, whole_rays), 0)
        )
        weight_slope = jnp.zeros((rays, STEPS), F32)
        color_rows = []
        decoded_slopes = []
        for channel in range(3):
            albedo = jax.nn.sigmoid(by_ray(1 + channel))
            color = jnp.sum(ray_weight * albedo, axis=1, keepdims=True)
            color_rows.append(jnp.sum(jnp.where(own_ray, color, 0.0), axis=0, keepdims=True))
            target = target_ref[channel : channel + 1, :]
            residual = color - jnp.sum(jnp.where(own_ray, target, 0.0), axis=1, keepdims=True)
            weight_slope = weight_slope + residual * albedo
            decoded_slopes.append(along_lanes(residual * ray_weight * albedo * (1.0 - albedo)))
        behind = jnp.dot(
            weight_slope * ray_weight,
            sum_behind,
            preferred_element_type=F32,
            precision=lax.Precision.HIGHEST,
        )
        optical_slope = weight_slope * through * passing - behind
        density_slope = optical_slope * DEPTH_STEP * jax.nn.sigmoid(raw_density)
        decoded_slope = jnp.concatenate([along_lanes(density_slope)] + decoded_slopes, axis=0)
        hidden2_slope = contract(w3_ref[...], decoded_slope.astype(BF16), 0, 0).astype(BF16)
        pre2_slope = hidden2_slope.astype(F32) * (gate2 * (1.0 + pre2 * (1.0 - gate2)))
        hidden1_slope = contract(w2_ref[...], pre2_slope.astype(BF16), 0, 0).astype(BF16)
        pre1_slope = hidden1_slope.astype(F32) * (gate1 * (1.0 + pre1 * (1.0 - gate1)))
        slope = contract(w1_ref[...], pre1_slope.astype(BF16), 0, 0).astype(BF16)
        return jnp.concatenate(color_rows, axis=0), slope

    colors_ref[...] = jnp.zeros(colors_ref.shape, F32)

    def render_part(part, _):
        colors, slope = shade(part, interpolate(part))
        colors_ref[...] += colors
        slope_ref[:, pl.ds(pl.multiple_of(part * tile, tile), tile)] = slope
        return 0

    lax.fori_loop(0, samples // tile, render_part, 0)

    def scatter(plane, _):
        slope = slope_ref[...]
        band_id = table_ref[plane, 0:1, :]
        spread = jnp.concatenate(
            [slope * jnp.where(band_id == q, 1.0, 0.0).astype(BF16) for q in range(bands)], axis=0
        )
        sums_ref[plane] = contract(spread, matrix_ref[plane], 1, 1)
        return 0

    lax.fori_loop(0, PLANES, scatter, 0)

    joined = []
    for plane in range(PLANES):
        rows = []
        for kind in range(2):
            parts, reached = [], 0
            for q in range(kind, bands, 2):
                start = q * stride
                lead = start % LANES
                piece = sums_ref[plane, q * channels : (q + 1) * channels, :]
                if lead:
                    piece = jnp.concatenate([piece, jnp.zeros((channels, LANES), F32)], axis=1)
                    piece = pltpu.roll(piece, lead, 1)
                if start - lead > reached:
                    parts.append(jnp.zeros((channels, start - lead - reached), F32))
                parts.append(piece)
                reached = start - lead + piece.shape[1]
            if plane_size > reached:
                parts.append(jnp.zeros((channels, plane_size - reached), F32))
            rows.append(jnp.concatenate(parts, axis=1))
        joined.append((rows[0] + rows[1]).astype(BF16))
    joined = jnp.concatenate(joined, axis=1)
    for i in range(shares):
        whole_ref[i] = joined[:, i * share : (i + 1) * share]
    for k in range(0, shares, 2):
        even_refs[k // 2][...] = whole_ref[me ^ k]
        odd_refs[k // 2][...] = whole_ref[me ^ (k + 1)]


def render_call(pieces, table, target, w1, b1, w2, b2, w3, b3):
    shares = len(pieces)
    channels, share = pieces[0].shape
    samples = table.shape[-1]
    grid_side = math.isqrt(shares * share // PLANES)
    row_span = band_span(grid_side)
    bands = (grid_side - 1) // row_span
    band = (row_span + 1) * grid_side
    tile = math.gcd(samples // STEPS, TILE_RAYS) * STEPS
    row = lambda array: array.reshape(1, -1)
    colors, *grads = pl.pallas_call(
        functools.partial(render_kernel, grid_side, row_span, shares, tile),
        out_shape=[
            jax.ShapeDtypeStruct(target.shape, F32),
            *[jax.ShapeDtypeStruct((channels, share), BF16)] * shares,
        ],
        scratch_shapes=[
            pltpu.VMEM((PLANES, bands * channels, band), BF16),
            pltpu.VMEM((PLANES, bands * channels, band), F32),
            pltpu.VMEM((PLANES, band, samples), BF16),
            pltpu.VMEM((shares, channels, share), BF16),
            pltpu.VMEM((channels, samples), BF16),
        ],
        compiler_params=params(),
        name="render",
    )(*pieces, table, target, w1, row(b1), w2, row(b2), w3, row(b3))
    return colors, grads[: shares // 2], grads[shares // 2 :]


def weight_grad_kernel(count, *refs):
    part_refs, refs = refs[:count], refs[count:]
    plane_in_ref, even_ref, odd_ref, grad_ref, total_ref, chunk_ref = refs
    step = pl.program_id(0)
    grad = part_refs[0][...].astype(F32)
    for ref in part_refs[1:]:
        grad = grad + ref[...].astype(F32)
    grad = grad.astype(BF16)
    grad_ref[...] = grad
    product = jnp.dot(grad, plane_in_ref[...], preferred_element_type=F32)

    @pl.when(step == 0)
    def begin():
        total_ref[...] = product

    @pl.when(step > 0)
    def add():
        total_ref[...] += product

    @pl.when(step == pl.num_programs(0) - 1)
    def cut():
        me = lax.axis_index("seq")
        shares, _, columns = chunk_ref.shape
        for i in range(shares):
            chunk_ref[i] = total_ref[:, i * columns : (i + 1) * columns]
        for j in range(shares // 2):
            even_ref[j] = chunk_ref[me ^ (2 * j)]
            odd_ref[j] = chunk_ref[me ^ (2 * j + 1)]


def weight_grad_call(parts, plane_in, shares):
    rows, width = plane_in.shape
    channels = parts[0].shape[0]
    columns = width // shares
    chunks = (shares // 2, channels, columns)
    tile = math.gcd(rows, 768)
    part_block = pl.BlockSpec((channels, tile), lambda step: (0, step))
    return pl.pallas_call(
        functools.partial(weight_grad_kernel, len(parts)),
        grid=(rows // tile,),
        in_specs=[
            *[part_block] * len(parts),
            pl.BlockSpec((tile, width), lambda step: (step, 0)),
        ],
        out_specs=[kept(chunks), kept(chunks), part_block],
        out_shape=[
            jax.ShapeDtypeStruct(chunks, F32),
            jax.ShapeDtypeStruct(chunks, F32),
            jax.ShapeDtypeStruct((channels, rows), BF16),
        ],
        scratch_shapes=[
            pltpu.VMEM((channels, width), F32),
            pltpu.VMEM((shares, channels, columns), F32),
        ],
        compiler_params=params(),
        name="weight_grad",
    )(*parts, plane_in)


def token_grad_kernel(grad_ref, w_plane_ref, token_grad_ref):
    token_grad_ref[...] = contract(grad_ref[...], w_plane_ref[...], 0, 0).astype(BF16)


def token_grad_call(grad, w_plane_t):
    channels, rows = grad.shape
    width = w_plane_t.shape[1]
    tile = math.gcd(rows, 384)
    return pl.pallas_call(
        token_grad_kernel,
        grid=(rows // tile,),
        in_specs=[
            pl.BlockSpec((channels, tile), lambda step: (0, step)),
            whole(w_plane_t.shape),
        ],
        out_specs=pl.BlockSpec((tile, width), lambda step: (step, 0)),
        out_shape=jax.ShapeDtypeStruct((rows, width), BF16),
        cost_estimate=estimate(2 * rows * width * channels, 2 * rows * width),
        compiler_params=params(16 * MIB),
        name="token_grad",
    )(grad, w_plane_t)


def join_kernel(count, *refs):
    chunk_refs, (out_ref, chunks_ref) = refs[:count], refs[count:]
    me = lax.axis_index("seq")
    columns = chunk_refs[0].shape[1]
    for k in range(count):
        chunks_ref[me ^ k] = chunk_refs[k][...]
    for i in range(count):
        out_ref[:, i * columns : (i + 1) * columns] = chunks_ref[i]


def join_call(chunks):
    channels, columns = chunks[0].shape
    return pl.pallas_call(
        functools.partial(join_kernel, len(chunks)),
        out_shape=jax.ShapeDtypeStruct((channels, columns * len(chunks)), F32),
        scratch_shapes=[pltpu.VMEM((len(chunks), channels, columns), F32)],
        compiler_params=params(),
        name="join_weight_grad",
    )(*chunks)


def body(
    tokens,
    image_tokens,
    norm_gain,
    w_query,
    w_key,
    w_value,
    w_out,
    w_plane,
    dec_w1,
    dec_b1,
    dec_w2,
    dec_b2,
    dec_w3,
    dec_b3,
    corner_idx,
    corner_wts,
    target_color,
):
    own_tokens = tokens[0]
    head_dim = own_tokens.shape[1] // HEADS
    query_scale = math.log2(math.e) / math.sqrt(head_dim)
    shares = lax.axis_size("seq")
    rows_here = own_tokens.shape[0]
    far_images = from_chips(image_tokens[0])
    images = with_other_core([image_tokens[0]])
    queries = query_call(own_tokens, w_query, query_scale)
    far_images, queries = lax.optimization_barrier((far_images, queries))
    images = images + with_other_core(far_images)
    w_plane_t = w_plane.T
    plane_in, planes = attend_call(
        images, w_key, w_value, own_tokens, queries, w_out, norm_gain, w_plane_t, head_dim
    )
    far_planes = from_chips(planes)
    planes = with_other_core([planes])
    table, target = corners_call(
        corner_idx[0], corner_wts[0], target_color[0], shares * rows_here
    )
    far_planes, table, target = lax.optimization_barrier((far_planes, table, target))
    colors, kept, passed = render_call(
        planes + with_other_core(far_planes),
        table,
        target,
        dec_w1,
        dec_b1,
        dec_w2,
        dec_b2,
        dec_w3,
        dec_b3,
    )
    parts = []
    for j in reversed(range(shares // 2)):
        pair = (kept[j].astype(F32) + swap(passed[j], "seq", 1).astype(F32)).astype(BF16)
        parts.append(swap(pair, "seq", 2 * j) if j else pair)
    kept, passed, grad = weight_grad_call(parts, plane_in, shares)
    pairs = kept + swap(passed, "seq", 1)
    chunk = pairs[0]
    for j in range(1, shares // 2):
        chunk = chunk + swap(pairs[j], "seq", 2 * j)
    others = [swap(chunk, "dp", k) for k in range(1, lax.axis_size("dp"))]
    token_grad = token_grad_call(grad, w_plane_t)
    others, token_grad = lax.optimization_barrier((others, token_grad))
    scenes = sum(others, chunk)
    weight_grad = join_call(gather_scene(scenes)).T
    return (colors[None], token_grad[None], weight_grad)


def solution(mesh):
    in_specs = (
        P("dp", "seq", None),
        P("dp", "seq", None),
        P(),
        P(),
        P(),
        P(),
        P(),
        P(),
        P(),
        P(),
        P(),
        P(),
        P(),
        P(),
        P("dp", None, "seq"),
        P("dp", None, "seq"),
        P("dp", None, "seq"),
    )
    out_specs = (P("dp", None, "seq"), P("dp", "seq", None), P())
    return jax.shard_map(body, mesh=mesh, in_specs=in_specs, out_specs=out_specs, check_vma=False)
```

```python
import functools
import math

import jax
import jax.numpy as jnp
from jax import lax
from jax.experimental import pallas as pl
from jax.experimental.pallas import tpu as pltpu
from jax.sharding import PartitionSpec as P

HEADS = 16
STEPS = 128
PLANES = 3
LANES = 128
TILE_RAYS = 32
TOGETHER = 8

NORM_EPS = 1e-05
DEPTH_STEP = 0.02
MIB = 1024 * 1024
VMEM_BYTES = 60 * MIB

F32 = jnp.float32
BF16 = jnp.bfloat16


def contract(left, right, left_dim, right_dim, out_type=F32, precision=None):
    return lax.dot_general(
        left,
        right,
        (((left_dim,), (right_dim,)), ((), ())),
        preferred_element_type=out_type,
        precision=precision,
    )


def plain_norm(inputs):
    row_mean = jnp.mean(inputs, axis=-1, keepdims=True)
    centred = inputs - row_mean
    row_var = jnp.mean(centred * centred, axis=-1, keepdims=True)
    return centred * lax.rsqrt(row_var + NORM_EPS)


def params(vmem_bytes=VMEM_BYTES):
    return pltpu.CompilerParams(vmem_limit_bytes=vmem_bytes)


def swap(array, axis, distance):
    pairs = [(i, i ^ distance) for i in range(lax.axis_size(axis))]
    return lax.ppermute(array, axis, pairs)


def from_chips(piece):
    far = {k: swap(piece, "seq", k) for k in reversed(range(2, lax.axis_size("seq"), 2))}
    return [far[k] for k in sorted(far)]


def with_other_core(pieces):
    return [each for piece in pieces for each in (piece, swap(piece, "seq", 1))]


def gather_scene(piece):
    return with_other_core([piece]) + with_other_core(from_chips(piece))


def whole(shape):
    return pl.BlockSpec(shape, lambda step: (0,) * len(shape), pipeline_mode=pl.Buffered(1))


def kept(shape):
    return pl.BlockSpec(shape, lambda step: (0,) * len(shape))


def estimate(flops, bytes_accessed):
    return pl.CostEstimate(flops=flops, bytes_accessed=bytes_accessed, transcendentals=0)


def query_kernel(query_scale, tokens_ref, w_query_ref, queries_ref):
    normed = plain_norm(tokens_ref[...].astype(F32)).astype(BF16)
    queries = jnp.dot(normed, w_query_ref[...], preferred_element_type=F32)
    queries_ref[...] = (queries * query_scale).astype(BF16)


def query_call(tokens, w_query, query_scale):
    rows, width = tokens.shape
    tile = math.gcd(rows, 512)
    return pl.pallas_call(
        functools.partial(query_kernel, query_scale),
        grid=(rows // tile,),
        in_specs=[pl.BlockSpec((tile, width), lambda step: (step, 0)), whole(w_query.shape)],
        out_specs=pl.BlockSpec((tile, width), lambda step: (step, 0)),
        out_shape=jax.ShapeDtypeStruct((rows, width), BF16),
        cost_estimate=estimate(2 * rows * width * width, 4 * rows * width),
        compiler_params=params(),
        name="queries",
    )(tokens, w_query)


def attend_kernel(head_dim, shares, *refs):
    image_refs, refs = refs[:shares], refs[shares:]
    w_key_ref, w_value_ref, tokens_ref, queries_ref, w_out_ref, gain_ref, w_plane_ref = refs[:7]
    plane_in_ref, planes_ref, keys_ref, values_ref, attended_ref = refs[7:]
    rows, width = tokens_ref.shape
    groups = width // LANES

    @pl.when(pl.program_id(0) == 0)
    def project_images():
        images = jnp.concatenate([ref[...] for ref in image_refs], axis=0)
        keys = jnp.dot(images, w_key_ref[...], preferred_element_type=F32).astype(BF16)
        keys_ref[...] = keys.T
        values = jnp.dot(images, w_value_ref[...], preferred_element_type=F32).astype(BF16)
        ones = jnp.ones((values.shape[0], LANES), BF16)
        for group in range(groups):
            values_ref[group, :, :LANES] = values[:, group * LANES : (group + 1) * LANES]
            values_ref[group, :, LANES:] = ones

    lane_ids = lax.broadcasted_iota(jnp.int32, (rows, LANES), 1)
    together = math.gcd(groups, TOGETHER)
    heads = [(group, low) for group in range(together) for low in range(0, LANES, head_dim)]

    def own_lanes(low):
        return (lane_ids >= low) & (lane_ids < low + head_dim)

    def group_step(step, _):
        def columns(group):
            return pl.ds(pl.multiple_of((step * together + group) * LANES, LANES), LANES)

        def head_scores(head):
            group, low = heads[head]
            group_queries = queries_ref[:, columns(group)]
            head_queries = jnp.where(own_lanes(low), group_queries, jnp.zeros_like(group_queries))
            return jnp.dot(
                head_queries, keys_ref[columns(group), :], preferred_element_type=F32
            )

        upcoming = head_scores(0)
        joined = None
        for head, (group, low) in enumerate(heads):
            scores = upcoming
            if head + 1 < len(heads):
                upcoming = head_scores(head + 1)
            row_max = jnp.max(scores, axis=1, keepdims=True)
            probs = jnp.exp2(scores - row_max).astype(BF16)
            sums = jnp.dot(
                probs, values_ref[step * together + group], preferred_element_type=F32
            )
            head_out = sums[:, :LANES] / sums[:, LANES:]
            joined = head_out if low == 0 else jnp.where(own_lanes(low), head_out, joined)
            if low + head_dim == LANES:
                attended_ref[:, columns(group)] = joined.astype(BF16)
        return 0

    lax.fori_loop(0, groups // together, group_step, 0)
    mixed = (
        tokens_ref[...].astype(F32)
        + jnp.dot(attended_ref[...], w_out_ref[...], preferred_element_type=F32)
    ).astype(BF16)
    plane_in = (plain_norm(mixed.astype(F32)) * gain_ref[...]).astype(BF16)
    plane_in_ref[...] = plane_in
    planes_ref[...] = contract(w_plane_ref[...], plane_in, 1, 1).astype(BF16)


def attend_call(images, w_key, w_value, tokens, queries, w_out, norm_gain, w_plane_t, head_dim):
    rows, width = tokens.shape
    channels = w_plane_t.shape[0]
    image_rows = sum(piece.shape[0] for piece in images)
    tile = math.gcd(rows, 384)
    row_block = pl.BlockSpec((tile, width), lambda step: (step, 0))
    return pl.pallas_call(
        functools.partial(attend_kernel, head_dim, len(images)),
        grid=(rows // tile,),
        in_specs=[
            *[whole(piece.shape) for piece in images],
            whole(w_key.shape),
            whole(w_value.shape),
            row_block,
            row_block,
            whole(w_out.shape),
            whole((1, width)),
            whole(w_plane_t.shape),
        ],
        out_specs=[row_block, pl.BlockSpec((channels, tile), lambda step: (0, step))],
        out_shape=[
            jax.ShapeDtypeStruct((rows, width), BF16),
            jax.ShapeDtypeStruct((channels, rows), BF16),
        ],
        scratch_shapes=[
            pltpu.VMEM((width, image_rows), BF16),
            pltpu.VMEM((width // LANES, image_rows, 2 * LANES), BF16),
            pltpu.VMEM((tile, width), BF16),
        ],
        cost_estimate=estimate(4 * rows * width * (image_rows + width // 2), 2 * rows * width),
        compiler_params=params(),
        name="attention_planes",
    )(*images, w_key, w_value, tokens, queries, w_out, norm_gain.reshape(1, width), w_plane_t)


def corners_kernel(
    grid_side, row_span, index_ref, weight_ref, target_ref, table_ref, target_out_ref
):
    target_out_ref[...] = target_ref[...]
    index = index_ref[...]
    weights = weight_ref[...].astype(F32)
    plane_size = grid_side * grid_side
    for plane in range(PLANES):
        in_plane = (index >= plane * plane_size) & (index < (plane + 1) * plane_size)
        base = jnp.min(jnp.where(in_plane, index, PLANES * plane_size), axis=0, keepdims=True)
        local = base - plane * plane_size
        first_row = local // grid_side
        band_id = first_row // row_span
        places = [band_id, first_row - band_id * row_span, local - first_row * grid_side]
        picked = [
            jnp.sum(jnp.where(index == base + shift, weights, 0.0), axis=0, keepdims=True)
            for shift in (0, 1, grid_side, grid_side + 1)
        ]
        rows = [place.astype(F32) for place in places] + picked + [jnp.zeros_like(picked[0])]
        table_ref[plane] = jnp.concatenate(rows, axis=0)


def corners_call(index, weights, target, tokens):
    samples = index.shape[1]
    grid_side = math.isqrt(tokens // PLANES)
    return pl.pallas_call(
        functools.partial(corners_kernel, grid_side, band_span(grid_side)),
        out_shape=[
            jax.ShapeDtypeStruct((PLANES, 8, samples), F32),
            jax.ShapeDtypeStruct(target.shape, F32),
        ],
        cost_estimate=estimate(1000 * samples, 100 * samples),
        compiler_params=params(16 * MIB),
        name="corners",
    )(index, weights, target)


def band_span(grid_side):
    return next(span for span in range(7, 0, -1) if (grid_side - 1) % span == 0)


def shifted_left(block, lanes):
    return pltpu.roll(block, block.shape[1] - lanes, 1) if lanes else block


def render_kernel(grid_side, row_span, shares, tile, *refs):
    piece_refs, refs = refs[:shares], refs[shares:]
    (table_ref, target_ref, w1_ref, b1_ref, w2_ref, b2_ref, w3_ref, b3_ref), refs = (
        refs[:8],
        refs[8:],
    )
    colors_ref, even_refs, odd_refs = (
        refs[0],
        refs[1 : 1 + shares // 2],
        refs[1 + shares // 2 : 1 + shares],
    )
    bands_ref, sums_ref, matrix_ref, whole_ref, slope_ref = refs[1 + shares :]
    me = lax.axis_index("seq")
    channels, share = piece_refs[0].shape
    samples = table_ref.shape[-1]
    plane_size = grid_side * grid_side
    band_rows = row_span + 1
    band = band_rows * grid_side
    stride = row_span * grid_side
    bands = (grid_side - 1) // row_span
    rays = tile // STEPS
    whole_rays = target_ref.shape[1]

    def column(row_ref):
        extent = row_ref.shape[1]
        on_diagonal = lax.broadcasted_iota(jnp.int32, (extent, extent), 0) == lax.broadcasted_iota(
            jnp.int32, (extent, extent), 1
        )
        return jnp.sum(jnp.where(on_diagonal, row_ref[...], 0.0), axis=1, keepdims=True)

    bias1, bias2, bias3 = column(b1_ref), column(b2_ref), column(b3_ref)
    earlier = lax.broadcasted_iota(jnp.int32, (STEPS, STEPS), 0)
    later = lax.broadcasted_iota(jnp.int32, (STEPS, STEPS), 1)
    sum_before = jnp.where(earlier < later, 1.0, 0.0)
    sum_behind = jnp.where(earlier > later, 1.0, 0.0)

    for k in range(shares):
        whole_ref[me ^ k] = piece_refs[k][...]
    whole_planes = jnp.concatenate([whole_ref[i] for i in range(shares)], axis=1)
    for plane in range(PLANES):
        for q in range(bands):
            start = plane * plane_size + q * stride
            lead = start % LANES
            extent = band + (LANES if lead else 0)
            piece = whole_planes[:, start - lead : start - lead + extent]
            if lead:
                piece = shifted_left(piece.astype(F32), lead).astype(BF16)
            bands_ref[plane, q * channels : (q + 1) * channels, :] = piece[:, :band]

    def interpolate(part):
        part_samples = pl.ds(pl.multiple_of(part * tile, tile), tile)
        features = jnp.zeros((channels, tile), F32)
        x_ids = lax.broadcasted_iota(jnp.int32, (grid_side, tile), 0).astype(F32)
        for plane in range(PLANES):
            band_id, band_row, first_x, *picked = (
                table_ref[plane, row : row + 1, part_samples] for row in range(7)
            )
            at_first = x_ids == first_x
            at_second = x_ids == first_x + 1.0
            upper = jnp.where(at_first, picked[0], jnp.where(at_second, picked[1], 0.0))
            lower = jnp.where(at_first, picked[2], jnp.where(at_second, picked[3], 0.0))
            upper, lower = upper.astype(BF16), lower.astype(BF16)
            marks = [jnp.where(band_row == r, 1.0, 0.0).astype(BF16) for r in range(row_span)]
            for r in range(band_rows):
                block = upper * marks[r] if r < row_span else None
                if r > 0:
                    below = lower * marks[r - 1]
                    block = below if block is None else block + below
                matrix_ref[plane, r * grid_side : (r + 1) * grid_side, part_samples] = block
            products = jnp.dot(
                bands_ref[plane], matrix_ref[plane, :, part_samples], preferred_element_type=F32
            )
            for q in range(bands):
                features = features + jnp.where(
                    band_id == q, products[q * channels : (q + 1) * channels, :], 0.0
                )
        return features.astype(BF16)

    def shade(part, features):
        pre1 = jnp.dot(w1_ref[...], features, preferred_element_type=F32) + bias1
        gate1 = jax.nn.sigmoid(pre1)
        hidden1 = (pre1 * gate1).astype(BF16)
        pre2 = jnp.dot(w2_ref[...], hidden1, preferred_element_type=F32) + bias2
        gate2 = jax.nn.sigmoid(pre2)
        hidden2 = (pre2 * gate2).astype(BF16)
        decoded = jnp.dot(w3_ref[...], hidden2, preferred_element_type=F32) + bias3

        def by_ray(row):
            return jnp.concatenate(
                [decoded[row : row + 1, i * STEPS : (i + 1) * STEPS] for i in range(rays)], axis=0
            )

        def along_lanes(by_rays):
            return jnp.concatenate([by_rays[i : i + 1, :] for i in range(rays)], axis=1)

        raw_density = by_ray(0)
        density = jnp.maximum(raw_density, 0.0) + jnp.log1p(jnp.exp(-jnp.abs(raw_density)))
        optical = density * DEPTH_STEP
        before = jnp.dot(
            optical, sum_before, preferred_element_type=F32, precision=lax.Precision.HIGHEST
        )
        through = jnp.exp(-before)
        passing = jnp.exp(-optical)
        ray_weight = through * (1.0 - passing)
        own_ray = lax.broadcasted_iota(jnp.int32, (rays, whole_rays), 1) == (
            part * rays + lax.broadcasted_iota(jnp.int32, (rays, whole_rays), 0)
        )
        weight_slope = jnp.zeros((rays, STEPS), F32)
        color_rows = []
        decoded_slopes = []
        for channel in range(3):
            albedo = jax.nn.sigmoid(by_ray(1 + channel))
            color = jnp.sum(ray_weight * albedo, axis=1, keepdims=True)
            color_rows.append(jnp.sum(jnp.where(own_ray, color, 0.0), axis=0, keepdims=True))
            target = target_ref[channel : channel + 1, :]
            residual = color - jnp.sum(jnp.where(own_ray, target, 0.0), axis=1, keepdims=True)
            weight_slope = weight_slope + residual * albedo
            decoded_slopes.append(along_lanes(residual * ray_weight * albedo * (1.0 - albedo)))
        behind = jnp.dot(
            weight_slope * ray_weight,
            sum_behind,
            preferred_element_type=F32,
            precision=lax.Precision.HIGHEST,
        )
        optical_slope = weight_slope * through * passing - behind
        density_slope = optical_slope * DEPTH_STEP * jax.nn.sigmoid(raw_density)
        decoded_slope = jnp.concatenate([along_lanes(density_slope)] + decoded_slopes, axis=0)
        hidden2_slope = contract(w3_ref[...], decoded_slope.astype(BF16), 0, 0).astype(BF16)
        pre2_slope = hidden2_slope.astype(F32) * (gate2 * (1.0 + pre2 * (1.0 - gate2)))
        hidden1_slope = contract(w2_ref[...], pre2_slope.astype(BF16), 0, 0).astype(BF16)
        pre1_slope = hidden1_slope.astype(F32) * (gate1 * (1.0 + pre1 * (1.0 - gate1)))
        slope = contract(w1_ref[...], pre1_slope.astype(BF16), 0, 0).astype(BF16)
        return jnp.concatenate(color_rows, axis=0), slope

    colors_ref[...] = jnp.zeros(colors_ref.shape, F32)

    def render_part(part, _):
        colors, slope = shade(part, interpolate(part))
        colors_ref[...] += colors
        slope_ref[:, pl.ds(pl.multiple_of(part * tile, tile), tile)] = slope
        return 0

    lax.fori_loop(0, samples // tile, render_part, 0)

    def scatter(plane, _):
        slope = slope_ref[...]
        band_id = table_ref[plane, 0:1, :]
        spread = jnp.concatenate(
            [slope * jnp.where(band_id == q, 1.0, 0.0).astype(BF16) for q in range(bands)], axis=0
        )
        sums_ref[plane] = contract(spread, matrix_ref[plane], 1, 1)
        return 0

    lax.fori_loop(0, PLANES, scatter, 0)

    joined = []
    for plane in range(PLANES):
        rows = []
        for kind in range(2):
            parts, reached = [], 0
            for q in range(kind, bands, 2):
                start = q * stride
                lead = start % LANES
                piece = sums_ref[plane, q * channels : (q + 1) * channels, :]
                if lead:
                    piece = jnp.concatenate([piece, jnp.zeros((channels, LANES), F32)], axis=1)
                    piece = pltpu.roll(piece, lead, 1)
                if start - lead > reached:
                    parts.append(jnp.zeros((channels, start - lead - reached), F32))
                parts.append(piece)
                reached = start - lead + piece.shape[1]
            if plane_size > reached:
                parts.append(jnp.zeros((channels, plane_size - reached), F32))
            rows.append(jnp.concatenate(parts, axis=1))
        joined.append((rows[0] + rows[1]).astype(BF16))
    joined = jnp.concatenate(joined, axis=1)
    for i in range(shares):
        whole_ref[i] = joined[:, i * share : (i + 1) * share]
    for k in range(0, shares, 2):
        even_refs[k // 2][...] = whole_ref[me ^ k]
        odd_refs[k // 2][...] = whole_ref[me ^ (k + 1)]


def render_call(pieces, table, target, w1, b1, w2, b2, w3, b3):
    shares = len(pieces)
    channels, share = pieces[0].shape
    samples = table.shape[-1]
    grid_side = math.isqrt(shares * share // PLANES)
    row_span = band_span(grid_side)
    bands = (grid_side - 1) // row_span
    band = (row_span + 1) * grid_side
    tile = math.gcd(samples // STEPS, TILE_RAYS) * STEPS
    row = lambda array: array.reshape(1, -1)
    colors, *grads = pl.pallas_call(
        functools.partial(render_kernel, grid_side, row_span, shares, tile),
        out_shape=[
            jax.ShapeDtypeStruct(target.shape, F32),
            *[jax.ShapeDtypeStruct((channels, share), BF16)] * shares,
        ],
        scratch_shapes=[
            pltpu.VMEM((PLANES, bands * channels, band), BF16),
            pltpu.VMEM((PLANES, bands * channels, band), F32),
            pltpu.VMEM((PLANES, band, samples), BF16),
            pltpu.VMEM((shares, channels, share), BF16),
            pltpu.VMEM((channels, samples), BF16),
        ],
        compiler_params=params(),
        name="render",
    )(*pieces, table, target, w1, row(b1), w2, row(b2), w3, row(b3))
    return colors, grads[: shares // 2], grads[shares // 2 :]


def weight_grad_kernel(count, *refs):
    part_refs, refs = refs[:count], refs[count:]
    plane_in_ref, even_ref, odd_ref, grad_ref, total_ref, chunk_ref = refs
    step = pl.program_id(0)
    grad = part_refs[0][...].astype(F32)
    for ref in part_refs[1:]:
        grad = grad + ref[...].astype(F32)
    grad = grad.astype(BF16)
    grad_ref[...] = grad
    product = jnp.dot(grad, plane_in_ref[...], preferred_element_type=F32)

    @pl.when(step == 0)
    def begin():
        total_ref[...] = product

    @pl.when(step > 0)
    def add():
        total_ref[...] += product

    @pl.when(step == pl.num_programs(0) - 1)
    def cut():
        me = lax.axis_index("seq")
        shares, _, columns = chunk_ref.shape
        for i in range(shares):
            chunk_ref[i] = total_ref[:, i * columns : (i + 1) * columns]
        for j in range(shares // 2):
            even_ref[j] = chunk_ref[me ^ (2 * j)]
            odd_ref[j] = chunk_ref[me ^ (2 * j + 1)]


def weight_grad_call(parts, plane_in, shares):
    rows, width = plane_in.shape
    channels = parts[0].shape[0]
    columns = width // shares
    chunks = (shares // 2, channels, columns)
    tile = math.gcd(rows, 768)
    part_block = pl.BlockSpec((channels, tile), lambda step: (0, step))
    return pl.pallas_call(
        functools.partial(weight_grad_kernel, len(parts)),
        grid=(rows // tile,),
        in_specs=[
            *[part_block] * len(parts),
            pl.BlockSpec((tile, width), lambda step: (step, 0)),
        ],
        out_specs=[kept(chunks), kept(chunks), part_block],
        out_shape=[
            jax.ShapeDtypeStruct(chunks, F32),
            jax.ShapeDtypeStruct(chunks, F32),
            jax.ShapeDtypeStruct((channels, rows), BF16),
        ],
        scratch_shapes=[
            pltpu.VMEM((channels, width), F32),
            pltpu.VMEM((shares, channels, columns), F32),
        ],
        compiler_params=params(),
        name="weight_grad",
    )(*parts, plane_in)


def token_grad_kernel(grad_ref, w_plane_ref, token_grad_ref):
    token_grad_ref[...] = contract(grad_ref[...], w_plane_ref[...], 0, 0).astype(BF16)


def token_grad_call(grad, w_plane_t):
    channels, rows = grad.shape
    width = w_plane_t.shape[1]
    tile = math.gcd(rows, 384)
    return pl.pallas_call(
        token_grad_kernel,
        grid=(rows // tile,),
        in_specs=[
            pl.BlockSpec((channels, tile), lambda step: (0, step)),
            whole(w_plane_t.shape),
        ],
        out_specs=pl.BlockSpec((tile, width), lambda step: (step, 0)),
        out_shape=jax.ShapeDtypeStruct((rows, width), BF16),
        cost_estimate=estimate(2 * rows * width * channels, 2 * rows * width),
        compiler_params=params(16 * MIB),
        name="token_grad",
    )(grad, w_plane_t)


def join_kernel(count, *refs):
    chunk_refs, (out_ref, chunks_ref) = refs[:count], refs[count:]
    me = lax.axis_index("seq")
    columns = chunk_refs[0].shape[1]
    for k in range(count):
        chunks_ref[me ^ k] = chunk_refs[k][...]
    for i in range(count):
        out_ref[:, i * columns : (i + 1) * columns] = chunks_ref[i]


def join_call(chunks):
    channels, columns = chunks[0].shape
    return pl.pallas_call(
        functools.partial(join_kernel, len(chunks)),
        out_shape=jax.ShapeDtypeStruct((channels, columns * len(chunks)), F32),
        scratch_shapes=[pltpu.VMEM((len(chunks), channels, columns), F32)],
        compiler_params=params(),
        name="join_weight_grad",
    )(*chunks)


def body(
    tokens,
    image_tokens,
    norm_gain,
    w_query,
    w_key,
    w_value,
    w_out,
    w_plane,
    dec_w1,
    dec_b1,
    dec_w2,
    dec_b2,
    dec_w3,
    dec_b3,
    corner_idx,
    corner_wts,
    target_color,
):
    own_tokens = tokens[0]
    head_dim = own_tokens.shape[1] // HEADS
    query_scale = math.log2(math.e) / math.sqrt(head_dim)
    shares = lax.axis_size("seq")
    rows_here = own_tokens.shape[0]
    far_images = from_chips(image_tokens[0])
    images = with_other_core([image_tokens[0]])
    queries = query_call(own_tokens, w_query, query_scale)
    far_images, queries = lax.optimization_barrier((far_images, queries))
    images = images + with_other_core(far_images)
    w_plane_t = w_plane.T
    plane_in, planes = attend_call(
        images, w_key, w_value, own_tokens, queries, w_out, norm_gain, w_plane_t, head_dim
    )
    far_planes = from_chips(planes)
    planes = with_other_core([planes])
    table, target = corners_call(
        corner_idx[0], corner_wts[0], target_color[0], shares * rows_here
    )
    far_planes, table, target = lax.optimization_barrier((far_planes, table, target))
    colors, kept, passed = render_call(
        planes + with_other_core(far_planes),
        table,
        target,
        dec_w1,
        dec_b1,
        dec_w2,
        dec_b2,
        dec_w3,
        dec_b3,
    )
    parts = []
    for j in reversed(range(shares // 2)):
        pair = (kept[j].astype(F32) + swap(passed[j], "seq", 1).astype(F32)).astype(BF16)
        parts.append(swap(pair, "seq", 2 * j) if j else pair)
    kept, passed, grad = weight_grad_call(parts, plane_in, shares)
    pairs = kept + swap(passed, "seq", 1)
    chunk = pairs[0]
    for j in reversed(range(1, shares // 2)):
        chunk = chunk + swap(pairs[j], "seq", 2 * j)
    others = [swap(chunk, "dp", k) for k in reversed(range(1, lax.axis_size("dp")))]
    token_grad = token_grad_call(grad, w_plane_t)
    others, token_grad = lax.optimization_barrier((others, token_grad))
    scenes = sum(others, chunk)
    weight_grad = join_call(gather_scene(scenes)).T
    return (colors[None], token_grad[None], weight_grad)


def solution(mesh):
    in_specs = (
        P("dp", "seq", None),
        P("dp", "seq", None),
        P(),
        P(),
        P(),
        P(),
        P(),
        P(),
        P(),
        P(),
        P(),
        P(),
        P(),
        P(),
        P("dp", None, "seq"),
        P("dp", None, "seq"),
        P("dp", None, "seq"),
    )
    out_specs = (P("dp", None, "seq"), P("dp", "seq", None), P())
    return jax.shard_map(body, mesh=mesh, in_specs=in_specs, out_specs=out_specs, check_vma=False)
```
